256 devices in a mesh: narrow: 8 (over y, core), wide: 32 (over x, z).
Axes of the slice: x: 4, y: 4, z: 8, core: 2. Of those that a mesh axis runs over, the one named last changes fastest.
Arguments:
- image_emb: bfloat16 [16384, 1024], P(('narrow', 'wide')), may hold values from -0.5 to 0.5
- text_emb: bfloat16 [16384, 1024], P(('wide', 'narrow')), may hold values from -0.5 to 0.5
- caption_group: int32 [16384], replicated, may hold values from 0 to 8191, as said below
Outputs:
- image_grad: float32 [16384, 1024], P(('narrow', 'wide'))
- text_grad: float32 [16384, 1024], P(('wide', 'narrow'))
The draws below stay inside these ranges and needn't reach their ends.
Inputs may be any that keep to these rules, and one draw needn't show every extreme that they name: `caption_group`: ids 0 and 8191 both occur.
All inputs are finite; a program needn't handle non-finite values.
Results may differ from the reference program's by a relative error of at most 0.002.
Values may be sent and summed in bfloat16 or wider, within the bound.
No kernel may reach another device: no remote copies, remote signals or barrier semaphores. Data moves between devices by JAX's collectives and lax.ppermute only.
A program may use at most 64 MiB of HBM per device.

```python
import math
import jax
import jax.numpy as jnp
from jax import lax

D = 1024
B = 16384


def caption_ids(key):
    ids = jax.random.randint(key, (B,), 0, B // 2, dtype=jnp.int32)
    place = jnp.arange(B, dtype=jnp.int32)
    ids = jnp.where(place == 0, 0, ids)
    ids = jnp.where(place == B - 1, B // 2 - 1, ids)
    return ids


def text_rows(key):
    ids = caption_ids(key)
    inner = jax.random.fold_in(key, 11)
    key_normal = jax.random.fold_in(inner, 0)
    key_scale = jax.random.fold_in(inner, 2)
    normal_part = jnp.clip(jax.random.normal(key_normal, (B // 2, D), jnp.float32), -4.0, 4.0)
    table = normal_part / math.sqrt(D)
    spread = jnp.exp(jax.random.uniform(key_scale, (B, 1), jnp.float32, math.log(0.4), math.log(2.0)))
    return jnp.take(table, ids, axis=0) * spread


def draw_caption_group(key, part):
    return caption_ids(key)


def draw_text_emb(key, part):
    base = text_rows(key)
    result = base
    return jnp.clip(result, -0.5, 0.5).astype(jnp.bfloat16)


def draw_image_emb(key, part):
    base = text_rows(key)
    key = jax.random.fold_in(key, 5)
    key_noise, key_scale = jax.random.split(key)
    noise = jnp.clip(jax.random.normal(key_noise, (B, D), jnp.float32), -4.0, 4.0)
    spread = jnp.exp(jax.random.uniform(key_scale, (B, 1), jnp.float32, math.log(0.4), math.log(2.0)))
    result = 0.15 * base + noise * spread / math.sqrt(D)
    return jnp.clip(result, -0.5, 0.5).astype(jnp.bfloat16)


def setup_inputs(seed: int = 0) -> dict:
    seeds = jax.random.split(jax.random.key(seed), 4)
    return {
        "image_emb": draw_image_emb(jax.random.fold_in(seeds[3], 71), 0),
        "text_emb": draw_text_emb(jax.random.fold_in(seeds[3], 71), 0),
        "caption_group": draw_caption_group(jax.random.fold_in(seeds[3], 71), 0),
    }


logit_scale = 100.0
floor_value = -1.0e30


def block_logits(rows, text_emb, row_index, caption_group):
    scores = logit_scale * jnp.dot(rows, text_emb.T, preferred_element_type=jnp.float32)
    count = caption_group.shape[0]
    col_index = jnp.arange(count, dtype=jnp.int32)
    row_group = jnp.take(caption_group, row_index)
    diagonal = row_index[:, None] == col_index[None, :]
    repeated = row_group[:, None] == caption_group[None, :]
    valid = jnp.logical_or(jnp.logical_not(repeated), diagonal)
    return scores, valid, diagonal


def reference(image_emb, text_emb, caption_group):
    total_rows = image_emb.shape[0]
    width = image_emb.shape[1]
    block = min(1024, total_rows)
    count = total_rows // block
    starts = jnp.arange(count, dtype=jnp.int32) * block

    def first_pass(carry, start):
        col_peak, col_total = carry
        rows = lax.dynamic_slice_in_dim(image_emb, start, block, 0)
        row_index = (start + jnp.arange(block, dtype=jnp.int32)).astype(jnp.int32)
        scores, valid, diagonal = block_logits(rows, text_emb, row_index, caption_group)
        kept = jnp.where(valid, scores, floor_value)
        row_peak = jnp.max(kept, axis=1)
        row_total = jnp.sum(jnp.where(valid, jnp.exp(kept - row_peak[:, None]), 0.0), axis=1)
        top = jnp.maximum(col_peak, jnp.max(kept, axis=0))
        block_total = jnp.sum(jnp.where(valid, jnp.exp(kept - top[None, :]), 0.0), axis=0)
        col_total = col_total * jnp.exp(col_peak - top) + block_total
        return (top, col_total), row_peak + jnp.log(row_total)

    init = (jnp.full((total_rows,), floor_value, jnp.float32), jnp.zeros((total_rows,), jnp.float32))
    (col_peak, col_total), row_lse = lax.scan(first_pass, init, starts)
    row_lse = row_lse.reshape(total_rows)
    col_lse = col_peak + jnp.log(col_total)

    def second_pass(text_sum, pieces):
        start, lse = pieces
        rows = lax.dynamic_slice_in_dim(image_emb, start, block, 0)
        row_index = (start + jnp.arange(block, dtype=jnp.int32)).astype(jnp.int32)
        scores, valid, diagonal = block_logits(rows, text_emb, row_index, caption_group)
        weight = jnp.exp(scores - lse[:, None]) + jnp.exp(scores - col_lse[None, :])
        grad = 0.5 * jnp.where(valid, weight, 0.0) - jnp.where(diagonal, 1.0, 0.0)
        grad = grad.astype(jnp.bfloat16)
        image_part = logit_scale * jnp.dot(grad, text_emb, preferred_element_type=jnp.float32)
        text_sum = text_sum + logit_scale * jnp.dot(grad.T, rows, preferred_element_type=jnp.float32)
        return text_sum, image_part

    text_grad, image_grad = lax.scan(second_pass, jnp.zeros((total_rows, width), jnp.float32), (starts, row_lse.reshape(count, block)))
    return image_grad.reshape(total_rows, width), text_grad
```

```python
import jax
import jax.numpy as jnp
from jax import lax
from jax.experimental import pallas as pl
from jax.experimental.pallas import tpu as pltpu
from jax.sharding import Mesh, PartitionSpec as P

logit_scale = 100.0
floor_value = -1e30
mib = 1024 * 1024

axes = ("y", "core", "x", "z")
plane = ("y", "x")


def shift(values, axis, step):
    size = lax.axis_size(axis)
    return lax.ppermute(values, axis, [(i, (i + step) % size) for i in range(size)])


def z_order(size):
    order = [size // 2]
    for step in range(size // 2 - 1, 0, -1):
        order += [step, size - step]
    return order


def spread_plane(values, count):
    return lax.all_to_all(jnp.broadcast_to(values[None], (count,) + values.shape), plane, 0, 0)


def stats_kernel(rows_ref, cols_ref, ri_ref, rg_ref, ci_ref, cg_ref, kept_ref, row_ref, col_ref, peak, total):
    step = pl.program_id(0)
    scores = logit_scale * lax.dot_general(
        rows_ref[...], cols_ref[...], (((1,), (1,)), ((), ())), preferred_element_type=jnp.float32
    )
    valid = jnp.logical_or(rg_ref[...] != cg_ref[...], ri_ref[...] == ci_ref[...])
    kept = jnp.where(valid, scores, floor_value)
    kept_ref[...] = kept

    row_peak = jnp.max(kept, axis=1, keepdims=True)
    row_total = jnp.sum(jnp.exp(kept - row_peak), axis=1, keepdims=True)
    row_lse = row_peak + jnp.log(row_total)
    row_ref[...] = jnp.broadcast_to(row_lse, (row_lse.shape[0], 128)).T[0:1, :]

    @pl.when(step == 0)
    def _():
        peak[...] = jnp.full_like(peak, floor_value)
        total[...] = jnp.zeros_like(total)

    old = peak[...]
    top = jnp.maximum(old, jnp.max(kept, axis=0, keepdims=True))
    summed = total[...] * jnp.exp(old - top) + jnp.sum(jnp.exp(kept - top), axis=0, keepdims=True)
    peak[...] = top
    total[...] = summed

    @pl.when(step == pl.num_programs(0) - 1)
    def _():
        col_ref[...] = top + jnp.log(summed)


def block_stats(rows, cols, ri, rg, ci, cg):
    n_rows, width = rows.shape
    n_cols = cols.shape[0]
    block = 256
    return pl.pallas_call(
        stats_kernel,
        grid=(n_rows // block,),
        in_specs=[
            pl.BlockSpec((block, width), lambda i: (i, 0)),
            pl.BlockSpec((n_cols, width), lambda i: (0, 0)),
            pl.BlockSpec((block, 1), lambda i: (i, 0)),
            pl.BlockSpec((block, 1), lambda i: (i, 0)),
            pl.BlockSpec((1, n_cols), lambda i: (0, 0)),
            pl.BlockSpec((1, n_cols), lambda i: (0, 0)),
        ],
        out_specs=[
            pl.BlockSpec((block, n_cols), lambda i: (i, 0)),
            pl.BlockSpec((1, block), lambda i: (0, i)),
            pl.BlockSpec((1, n_cols), lambda i: (0, 0)),
        ],
        out_shape=[
            jax.ShapeDtypeStruct((n_rows, n_cols), jnp.float32),
            jax.ShapeDtypeStruct((1, n_rows), jnp.float32),
            jax.ShapeDtypeStruct((1, n_cols), jnp.float32),
        ],
        scratch_shapes=[pltpu.VMEM((1, n_cols), jnp.float32), pltpu.VMEM((1, n_cols), jnp.float32)],
        compiler_params=pltpu.CompilerParams(vmem_limit_bytes=32 * mib),
        cost_estimate=pl.CostEstimate(
            flops=2 * n_rows * n_cols * width, bytes_accessed=8 * mib, transcendentals=2 * n_rows * n_cols
        ),
        name="stats",
    )(rows, cols, ri, rg, ci, cg)


def merge(parts):
    top = jnp.max(parts, axis=0, keepdims=True)
    return top + jnp.log(jnp.sum(jnp.exp(parts - top), axis=0, keepdims=True))


def grad_kernel(kept_ref, rows_ref, row_parts, col_parts, ri_ref, ci_ref, grad_ref, text_ref):
    step = pl.program_id(0)
    row_lse = merge(row_parts[...])
    row_lse = jnp.broadcast_to(row_lse, (128, row_lse.shape[1])).T[:, 0:1]
    col_lse = merge(col_parts[...])
    kept = kept_ref[...]
    weight = jnp.exp(kept - row_lse) + jnp.exp(kept - col_lse)
    grad = 0.5 * weight - jnp.where(ri_ref[...] == ci_ref[...], 1.0, 0.0)
    grad = grad.astype(jnp.bfloat16)
    grad_ref[...] = grad
    part = lax.dot_general(grad, rows_ref[...], (((0,), (0,)), ((), ())), preferred_element_type=jnp.float32)

    @pl.when(step == 0)
    def _():
        text_ref[...] = part

    @pl.when(step > 0)
    def _():
        text_ref[...] += part


def block_grad(kept, rows, row_parts, col_parts, ri, ci):
    n_rows, width = rows.shape
    n_cols = kept.shape[1]
    block = 256
    return pl.pallas_call(
        grad_kernel,
        grid=(n_rows // block,),
        in_specs=[
            pl.BlockSpec((block, n_cols), lambda i: (i, 0)),
            pl.BlockSpec((block, width), lambda i: (i, 0)),
            pl.BlockSpec((row_parts.shape[0], block), lambda i: (0, i)),
            pl.BlockSpec((col_parts.shape[0], n_cols), lambda i: (0, 0)),
            pl.BlockSpec((block, 1), lambda i: (i, 0)),
            pl.BlockSpec((1, n_cols), lambda i: (0, 0)),
        ],
        out_specs=[
            pl.BlockSpec((block, n_cols), lambda i: (i, 0)),
            pl.BlockSpec((n_cols, width), lambda i: (0, 0)),
        ],
        out_shape=[
            jax.ShapeDtypeStruct((n_rows, n_cols), jnp.bfloat16),
            jax.ShapeDtypeStruct((n_cols, width), jnp.float32),
        ],
        compiler_params=pltpu.CompilerParams(vmem_limit_bytes=32 * mib),
        cost_estimate=pl.CostEstimate(
            flops=2 * n_rows * n_cols * width, bytes_accessed=12 * mib, transcendentals=2 * n_rows * n_cols
        ),
        name="grad",
    )(kept, rows, row_parts, col_parts, ri, ci)


def per_device(image_emb, text_emb, caption_group):
    span, width = image_emb.shape
    n_y, n_core, n_x, n_z = (lax.axis_size(a) for a in axes)
    y, core, x, z = (lax.axis_index(a) for a in axes)
    n_plane = n_y * n_x
    place = jnp.arange(span, dtype=jnp.int32)

    rows = spread_plane(image_emb, n_plane).reshape(n_plane * span, width)
    near = {0: text_emb}
    for step in z_order(n_z):
        near[step] = shift(text_emb, "z", -step)
    near = jnp.concatenate([near[k] for k in range(n_z)], axis=0)
    far = shift(near, "core", 1)
    cols = jnp.concatenate([near, far], axis=0)

    at_y = jnp.arange(n_y, dtype=jnp.int32)[:, None, None]
    at_x = jnp.arange(n_x, dtype=jnp.int32)[None, :, None]
    row_index = ((((at_y * n_core + core) * n_x + at_x) * n_z + z) * span + place).reshape(-1)
    at_core = jnp.stack([core, 1 - core])[:, None, None]
    at_z = ((z + jnp.arange(n_z, dtype=jnp.int32)) % n_z)[None, :, None]
    col_index = ((((x * n_z + at_z) * n_y + y) * n_core + at_core) * span + place).reshape(-1)
    blocks = caption_group.reshape(-1, span)
    row_group = jnp.take(blocks, row_index[::span] // span, axis=0).reshape(-1)
    col_group = jnp.take(blocks, col_index[::span] // span, axis=0).reshape(-1)
    ri, rg = row_index[:, None], row_group[:, None]
    ci, cg = col_index[None, :], col_group[None, :]

    kept, row_part, col_part = block_stats(rows, cols, ri, rg, ci, cg)
    row_parts = spread_plane(row_part[0], n_plane)
    own = col_part.reshape(n_core, n_z, span)
    other = shift(jnp.flip(own, axis=0), "core", 1)
    pair = jnp.stack([own, other])
    doubled = jnp.concatenate([pair, pair], axis=2)
    start = (n_z - z) % n_z
    common = lax.dynamic_slice_in_dim(doubled, start, n_z, axis=2)
    parts = lax.all_to_all(jnp.broadcast_to(common[None], (n_z,) + common.shape), "z", 0, 0)
    parts = parts.reshape(n_z * n_core, n_core, n_z, span)
    parts = lax.dynamic_slice_in_dim(jnp.concatenate([parts, parts], axis=2), z, n_z, axis=2)
    col_parts = parts.reshape(n_z * n_core, -1)

    grad, text_part = block_grad(kept, rows, row_parts, col_parts, ri, ci)
    half = n_z * span
    text_part = text_part[:half] + shift(text_part[half:], "core", 1)
    image_part = jnp.dot(grad, cols, preferred_element_type=jnp.float32)
    image_parts = lax.all_to_all(
        image_part.astype(jnp.bfloat16).reshape(n_plane, span, width), plane, 0, 0
    )
    image_grad = logit_scale * jnp.sum(image_parts.astype(jnp.float32), axis=0)
    text_part = text_part.reshape(n_z, span, width)
    text_sent = text_part.astype(jnp.bfloat16)
    text_grad = text_part[0]
    for step in z_order(n_z):
        text_grad = text_grad + shift(text_sent[step], "z", step).astype(jnp.float32)
    return (image_grad, logit_scale * text_grad)


def solution(mesh):
    fine = Mesh(mesh.devices.reshape(4, 2, 4, 8), axes)
    return jax.shard_map(
        per_device,
        mesh=fine,
        in_specs=(P(axes, None), P(("x", "z", "y", "core"), None), P()),
        out_specs=(P(axes, None), P(("x", "z", "y", "core"), None)),
        check_vma=False,
    )
```

```python
import jax
import jax.numpy as jnp
from jax import lax
from jax.experimental import pallas as pl
from jax.experimental.pallas import tpu as pltpu
from jax.sharding import Mesh, PartitionSpec as P

logit_scale = 100.0
floor_value = -1e30
mib = 1024 * 1024
lanes = 128
block = 256

axes = ("y", "core", "x", "z")
plane = ("y", "x")
pair_line = ("core", "z")


def swap_core(values):
    return lax.ppermute(values, "core", [(0, 1), (1, 0)])


def shift_z(values, step):
    size = lax.axis_size("z")
    return lax.ppermute(values, "z", [(i, (i + step) % size) for i in range(size)])


def z_steps(size):
    steps = [size // 2]
    for step in range(size // 2 - 1, 0, -1):
        steps += [step, size - step]
    return steps


def spread(values, axis, count):
    return lax.all_to_all(jnp.broadcast_to(values[None], (count,) + values.shape), axis, 0, 0)


def contract(a, b, dim_a, dim_b):
    return lax.dot_general(a, b, (((dim_a,), (dim_b,)), ((), ())), preferred_element_type=jnp.float32)


def as_column(row):
    return jnp.broadcast_to(row, (lanes, row.shape[1])).T[:, 0:1]


def as_row(column):
    return jnp.broadcast_to(column, (column.shape[0], lanes)).T[0:1, :]


def fold(row):
    return jnp.concatenate([row[:, i : i + lanes] for i in range(0, row.shape[1], lanes)], axis=0)


def unfold(tile):
    return jnp.concatenate([tile[i : i + 1, :] for i in range(tile.shape[0])], axis=1)


def by_core(tile, core):
    half = tile.shape[0] // 2
    return jnp.where(core == 0, tile, jnp.concatenate([tile[half:], tile[:half]], axis=0))


def stats_kernel(core, rows_ref, near_ref, far_ref, ri, rg, ci, cg, kept_ref, row_ref, col_ref, peak, total):
    step = pl.program_id(0)
    half = near_ref.shape[0]
    for side, ref in enumerate((near_ref, far_ref)):
        span = slice(side * half, (side + 1) * half)
        scores = logit_scale * contract(rows_ref[...], ref[...], 1, 1)
        valid = jnp.logical_or(rg[...] != cg[:, span], ri[...] == ci[:, span])
        kept_ref[:, span] = jnp.where(valid, scores, floor_value)
    kept = kept_ref[...]

    row_peak = jnp.max(kept, axis=1, keepdims=True)
    row_total = jnp.sum(jnp.exp(kept - row_peak), axis=1, keepdims=True)
    row_lse = as_row(row_peak + jnp.log(row_total))
    for i in range(block // lanes):
        piece = row_lse[:, i * lanes : (i + 1) * lanes]
        row_ref[:, pl.ds(step * (block // lanes) + i, 1), :] = jnp.broadcast_to(
            piece[None], (row_ref.shape[0], 1, lanes)
        )

    @pl.when(step == 0)
    def _():
        peak[...] = jnp.full_like(peak, floor_value)
        total[...] = jnp.zeros_like(total)

    old = peak[...]
    top = jnp.maximum(old, jnp.max(kept, axis=0, keepdims=True))
    summed = total[...] * jnp.exp(old - top) + jnp.sum(jnp.exp(kept - top), axis=0, keepdims=True)
    peak[...] = top
    total[...] = summed

    @pl.when(step == pl.num_programs(0) - 1)
    def _():
        col_lse = by_core(fold(top + jnp.log(summed)), core[0])
        col_ref[...] = jnp.broadcast_to(col_lse[None], col_ref.shape)


def whole(shape):
    return pl.BlockSpec(shape, lambda i: (0,) * len(shape))


def by_rows(width):
    return pl.BlockSpec((block, width), lambda i: (i, 0))


def block_stats(core, rows, near, far, ri, rg, ci, cg, n_row, n_col):
    n_rows, width = rows.shape
    n_cols = 2 * near.shape[0]
    return pl.pallas_call(
        stats_kernel,
        grid=(n_rows // block,),
        in_specs=[
            pl.BlockSpec(memory_space=pltpu.SMEM),
            by_rows(width),
            whole(near.shape),
            whole(far.shape),
            by_rows(1),
            by_rows(1),
            whole((1, n_cols)),
            whole((1, n_cols)),
        ],
        out_specs=[
            by_rows(n_cols),
            whole((n_row, n_rows // lanes, lanes)),
            whole((n_col, n_cols // lanes, lanes)),
        ],
        out_shape=[
            jax.ShapeDtypeStruct((n_rows, n_cols), jnp.float32),
            jax.ShapeDtypeStruct((n_row, n_rows // lanes, lanes), jnp.float32),
            jax.ShapeDtypeStruct((n_col, n_cols // lanes, lanes), jnp.float32),
        ],
        scratch_shapes=[pltpu.VMEM((1, n_cols), jnp.float32), pltpu.VMEM((1, n_cols), jnp.float32)],
        compiler_params=pltpu.CompilerParams(vmem_limit_bytes=20 * mib),
        cost_estimate=pl.CostEstimate(
            flops=2 * n_rows * n_cols * width, bytes_accessed=8 * mib, transcendentals=2 * n_rows * n_cols
        ),
        name="stats",
    )(core, rows, near, far, ri, rg, ci, cg)


def merge(parts):
    top = jnp.max(parts, axis=0)
    return top + jnp.log(jnp.sum(jnp.exp(parts - top[None]), axis=0))


def grad_kernel(core, kept_ref, near_ref, far_ref, row_parts, col_parts, ri, ci, grad_ref, image_ref):
    step = pl.program_id(0)
    half = near_ref.shape[0]
    per = block // lanes
    row_lse = as_column(unfold(merge(row_parts[:, pl.ds(step * per, per), :])))
    col_lse = unfold(by_core(merge(col_parts[...]), core[0]))
    kept = kept_ref[...]
    weight = jnp.exp(kept - row_lse) + jnp.exp(kept - col_lse)
    grad = 0.5 * weight - jnp.where(ri[...] == ci[...], 1.0, 0.0)
    grad = grad.astype(jnp.bfloat16)
    grad_ref[...] = grad
    part = contract(grad[:, :half], near_ref[...], 1, 0) + contract(grad[:, half:], far_ref[...], 1, 0)
    image_ref[...] = part.astype(jnp.bfloat16)


def block_grad(core, kept, near, far, row_parts, col_parts, ri, ci):
    n_rows, n_cols = kept.shape
    width = near.shape[1]
    return pl.pallas_call(
        grad_kernel,
        grid=(n_rows // block,),
        in_specs=[
            pl.BlockSpec(memory_space=pltpu.SMEM),
            by_rows(n_cols),
            whole(near.shape),
            whole(far.shape),
            whole(row_parts.shape),
            whole(col_parts.shape),
            by_rows(1),
            whole((1, n_cols)),
        ],
        out_specs=[by_rows(n_cols), by_rows(width)],
        out_shape=[
            jax.ShapeDtypeStruct((n_rows, n_cols), jnp.bfloat16),
            jax.ShapeDtypeStruct((n_rows, width), jnp.bfloat16),
        ],
        compiler_params=pltpu.CompilerParams(vmem_limit_bytes=20 * mib),
        cost_estimate=pl.CostEstimate(
            flops=2 * n_rows * n_cols * width, bytes_accessed=10 * mib, transcendentals=2 * n_rows * n_cols
        ),
        name="grad",
    )(core, kept, near, far, row_parts, col_parts, ri, ci)


def far_kernel(grad_ref, rows_ref, out_ref):
    out_ref[...] = contract(grad_ref[...], rows_ref[...], 0, 0)


def far_terms(grad, rows):
    n_rows, width = rows.shape
    n_cols = grad.shape[1] // 2
    skip = n_cols // block
    return pl.pallas_call(
        far_kernel,
        grid=(n_cols // block,),
        in_specs=[pl.BlockSpec((n_rows, block), lambda i: (0, i + skip)), whole(rows.shape)],
        out_specs=by_rows(width),
        out_shape=jax.ShapeDtypeStruct((n_cols, width), jnp.float32),
        compiler_params=pltpu.CompilerParams(vmem_limit_bytes=20 * mib),
        cost_estimate=pl.CostEstimate(
            flops=2 * n_rows * n_cols * width, bytes_accessed=5 * mib, transcendentals=0
        ),
        name="far_terms",
    )(grad, rows)


def text_kernel(z, grad_ref, rows_ref, other_ref, own_ref, *outs):
    sent, total = outs[:-1], outs[-1]
    span = own_ref.shape[0]
    n_z = len(sent) + 1
    step = pl.program_id(0)
    total[pl.ds(step * block, block), :] = contract(grad_ref[...], rows_ref[...], 0, 0) + other_ref[...]

    @pl.when(step == pl.num_programs(0) - 1)
    def _():
        for k in range(n_z):
            at = pl.multiple_of(lax.rem(z[0] + k, n_z) * span, span)
            value = total[pl.ds(at, span), :]
            if k == 0:
                own_ref[...] = value
            else:
                sent[k - 1][...] = value.astype(jnp.bfloat16)


def text_terms(z, grad, rows, other, n_z):
    n_rows, width = rows.shape
    n_cols = grad.shape[1] // 2
    span = n_cols // n_z
    return pl.pallas_call(
        text_kernel,
        grid=(n_cols // block,),
        in_specs=[
            pl.BlockSpec(memory_space=pltpu.SMEM),
            pl.BlockSpec((n_rows, block), lambda i: (0, i)),
            whole(rows.shape),
            by_rows(width),
        ],
        out_specs=[whole((span, width))] * n_z,
        out_shape=[jax.ShapeDtypeStruct((span, width), jnp.float32)]
        + [jax.ShapeDtypeStruct((span, width), jnp.bfloat16)] * (n_z - 1),
        scratch_shapes=[pltpu.VMEM((n_cols, width), jnp.float32)],
        compiler_params=pltpu.CompilerParams(vmem_limit_bytes=20 * mib),
        cost_estimate=pl.CostEstimate(
            flops=2 * n_rows * n_cols * width, bytes_accessed=6 * mib, transcendentals=0
        ),
        name="text_terms",
    )(z, grad, rows, other)


def sum_kernel(image_parts, own_ref, *refs):
    text_parts, (image_ref, text_ref) = refs[:-2], refs[-2:]
    image_ref[...] = logit_scale * jnp.sum(image_parts[...].astype(jnp.float32), axis=0)
    total = own_ref[...]
    for ref in text_parts:
        total = total + ref[...].astype(jnp.float32)
    text_ref[...] = logit_scale * total


def final_sums(image_parts, own, text_parts):
    n_plane, span, width = image_parts.shape
    tall = 16
    rows = pl.BlockSpec((tall, width), lambda i: (i, 0))
    return pl.pallas_call(
        sum_kernel,
        grid=(span // tall,),
        in_specs=[pl.BlockSpec((n_plane, tall, width), lambda i: (0, i, 0))] + [rows] * (1 + len(text_parts)),
        out_specs=[rows, rows],
        out_shape=[jax.ShapeDtypeStruct((span, width), jnp.float32)] * 2,
        compiler_params=pltpu.CompilerParams(vmem_limit_bytes=20 * mib),
        cost_estimate=pl.CostEstimate(flops=span * width * 24, bytes_accessed=4 * mib, transcendentals=0),
        name="sums",
    )(image_parts, own, *text_parts)


def join_kernel(z, *refs):
    shards, out_ref = refs[:-1], refs[-1]
    span = shards[0].shape[0]
    for k, ref in enumerate(shards):
        at = pl.multiple_of(lax.rem(z[0] + k, len(shards)) * span, span)
        out_ref[pl.ds(at, span), :] = ref[...]


def join(z, shards):
    span, width = shards[0].shape
    memory = pl.BlockSpec(memory_space=pltpu.VMEM)
    return pl.pallas_call(
        join_kernel,
        in_specs=[pl.BlockSpec(memory_space=pltpu.SMEM)] + [memory] * len(shards),
        out_specs=memory,
        out_shape=jax.ShapeDtypeStruct((len(shards) * span, width), shards[0].dtype),
        compiler_params=pltpu.CompilerParams(vmem_limit_bytes=8 * mib),
        cost_estimate=pl.CostEstimate(flops=0, bytes_accessed=2 * mib, transcendentals=0),
        name="join",
    )(z, *shards)


def per_device(image_emb, text_emb, caption_group):
    span, width = image_emb.shape
    n_y, n_core, n_x, n_z = (lax.axis_size(a) for a in axes)
    y, core, x, z = (lax.axis_index(a) for a in axes)
    n_plane = n_y * n_x
    place = jnp.arange(span, dtype=jnp.int32)
    z_scalar = z.reshape(1).astype(jnp.int32)
    core_scalar = core.reshape(1).astype(jnp.int32)

    rows = spread(image_emb, plane, n_plane).reshape(n_plane * span, width)
    shards = {0: text_emb}
    for k in z_steps(n_z):
        shards[k] = shift_z(text_emb, -k)
    near = join(z_scalar, [shards[k] for k in range(n_z)])
    far = swap_core(near)

    at_y = jnp.arange(n_y, dtype=jnp.int32)[:, None, None]
    at_x = jnp.arange(n_x, dtype=jnp.int32)[None, :, None]
    row_index = ((((at_y * n_core + core) * n_x + at_x) * n_z + z) * span + place).reshape(-1)
    at_core = jnp.stack([core, 1 - core])[:, None, None]
    at_z = jnp.arange(n_z, dtype=jnp.int32)[None, :, None]
    col_index = ((((x * n_z + at_z) * n_y + y) * n_core + at_core) * span + place).reshape(-1)
    blocks = caption_group.reshape(-1, span)
    row_group = jnp.take(blocks, row_index[::span] // span, axis=0).reshape(-1)
    col_group = jnp.take(blocks, col_index[::span] // span, axis=0).reshape(-1)
    ri, rg = row_index[:, None], row_group[:, None]
    ci, cg = col_index[None, :], col_group[None, :]

    kept, row_part, col_part = block_stats(
        core_scalar, rows, near, far, ri, rg, ci, cg, n_plane, n_z * n_core
    )
    row_parts = lax.all_to_all(row_part, plane, 0, 0)
    col_parts = lax.all_to_all(col_part, pair_line, 0, 0)

    grad, image_part = block_grad(core_scalar, kept, near, far, row_parts, col_parts, ri, ci)
    image_parts = lax.all_to_all(image_part.reshape(n_plane, span, width), plane, 0, 0)
    other = swap_core(far_terms(grad, rows))
    own, *sent = text_terms(z_scalar, grad, rows, other, n_z)
    text_parts = {k: shift_z(sent[k - 1], k) for k in z_steps(n_z)}
    image_grad, text_grad = final_sums(image_parts, own, [text_parts[k] for k in range(1, n_z)])
    return (image_grad, text_grad)


def solution(mesh):
    fine = Mesh(mesh.devices.reshape(4, 2, 4, 8), axes)
    return jax.shard_map(
        per_device,
        mesh=fine,
        in_specs=(P(axes, None), P(("x", "z", "y", "core"), None), P()),
        out_specs=(P(axes, None), P(("x", "z", "y", "core"), None)),
        check_vma=False,
    )
```

```python
import math

import jax
import jax.numpy as jnp
from jax import lax
from jax.experimental import pallas as pl
from jax.experimental.pallas import tpu as pltpu
from jax.sharding import Mesh, PartitionSpec as P

logit_scale = 100.0
scale_base2 = logit_scale / math.log(2.0)
floor_value = -1e30
mib = 1024 * 1024
lanes = 128
block = 256

axes = ("y", "core", "x", "z")
plane = ("y", "x")
in_vmem = pl.BlockSpec(memory_space=pltpu.VMEM)
in_hbm = pl.BlockSpec(memory_space=pltpu.HBM)


def swap_core(values):
    return lax.ppermute(values, "core", [(0, 1), (1, 0)])


def shift(values, axis, step):
    size = lax.axis_size(axis)
    return lax.ppermute(values, axis, [(i, (i + step) % size) for i in range(size)])


def shift_z(values, step):
    return shift(values, "z", step)


def z_steps(size):
    steps = [size // 2]
    for step in range(size // 2 - 1, 0, -1):
        steps += [step, size - step]
    return steps


def contract(a, b, dim_a, dim_b):
    return lax.dot_general(a, b, (((dim_a,), (dim_b,)), ((), ())), preferred_element_type=jnp.float32)


def as_column(row):
    return jnp.broadcast_to(row, (lanes, row.shape[1])).T[:, 0:1]


def as_row(column):
    return jnp.broadcast_to(column, (column.shape[0], lanes)).T[0:1, :]


def fold(row):
    return jnp.concatenate([row[:, i : i + lanes] for i in range(0, row.shape[1], lanes)], axis=0)


def unfold(tile):
    return jnp.concatenate([tile[i : i + 1, :] for i in range(tile.shape[0])], axis=1)


def by_core(tile, core):
    half = tile.shape[0] // 2
    return jnp.where(core == 0, tile, jnp.concatenate([tile[half:], tile[:half]], axis=0))


def estimate(flops, megabytes, exps=0):
    return pl.CostEstimate(flops=flops, bytes_accessed=megabytes * mib, transcendentals=exps)


def params(megabytes):
    return pltpu.CompilerParams(vmem_limit_bytes=megabytes * mib)


def here_in_mesh():
    return [lax.axis_index(name) for name in axes]


def row_ids(place, start, count, span):
    y, core, x, z = place
    at = start + lax.broadcasted_iota(jnp.int32, (count, 1), 0)
    member = at // span
    n_x, n_z, n_core = 4, 8, 2
    return (((member // n_x * n_core + core) * n_x + member % n_x) * n_z + z) * span + at % span


def col_ids(place, count, span):
    y, core, x, z = place
    n_y, n_z, n_core = 4, 8, 2
    at = lax.broadcasted_iota(jnp.int32, (1, count), 1)
    part = at // span
    side = jnp.where(part < n_z, core, 1 - core)
    return (((x * n_z + part % n_z) * n_y + y) * n_core + side) * span + at % span


def halves(a, b, which):
    low = lax.broadcasted_iota(jnp.int32, a.shape, 1) < lanes // 2
    turned_a = jnp.where(which == 0, a, pltpu.roll(a, lanes // 2, 1))
    turned_b = jnp.where(which == 0, pltpu.roll(b, lanes // 2, 1), b)
    return jnp.where(low, turned_a, turned_b)


def group_rows(place, group_ref):
    y, core, x, z = place
    n_x, n_z, n_plane = 4, 8, 16

    def ids(at):
        return group_ref[pl.ds(at, 1), :].astype(jnp.float32)

    rows = []
    for j in range(n_plane // 2):
        a, b = [ids(((m // n_x) * 2 + core) * 16 + (m % n_x) * 4 + z // 2) for m in (2 * j, 2 * j + 1)]
        rows.append(halves(a, b, lax.rem(z, 2)))
    cols = []
    for side in (core, 1 - core):
        for j in range(n_z // 2):
            a, b = [ids((x * n_z + m) * 4 + y) for m in (2 * j, 2 * j + 1)]
            cols.append(halves(a, b, side))
    return rows, cols


def repeat_kernel(in_ref, out_ref, held, sems):
    load = pltpu.make_async_copy(in_ref, held, sems.at[0])
    load.start()
    load.wait()
    copies = [pltpu.make_async_copy(held, out_ref.at[i], sems.at[1 + i]) for i in range(out_ref.shape[0])]
    for copy in copies:
        copy.start()
    for copy in copies:
        copy.wait()


def repeat(values, count):
    return pl.pallas_call(
        repeat_kernel,
        in_specs=[in_hbm],
        out_specs=in_hbm,
        out_shape=jax.ShapeDtypeStruct((count,) + values.shape, values.dtype),
        scratch_shapes=[pltpu.VMEM(values.shape, values.dtype), pltpu.SemaphoreType.DMA((1 + count,))],
        compiler_params=params(60),
        cost_estimate=estimate(0, 2),
        name="repeat",
    )(values)


def stats_kernel(rows, group_ref, *refs):
    shards, (kept_ref, cols_ref, row_ref, col_ref, kept_all, cols, groups, sems) = refs[:-8], refs[-8:]
    where = here_in_mesh()
    n_rows, n_cols = kept_ref.shape
    half = n_cols // 2
    n_blocks = n_rows // block
    n_z = len(shards) // 2
    span = half // n_z

    stores = [
        pltpu.make_async_copy(
            kept_all.at[pl.ds(i * block, block), :], kept_ref.at[pl.ds(i * block, block), :], sems.at[i]
        )
        for i in range(n_blocks)
    ]
    cols_store = pltpu.make_async_copy(cols, cols_ref, sems.at[n_blocks])
    group_load = pltpu.make_async_copy(group_ref, groups, sems.at[n_blocks + 1])
    group_load.start()
    for side in range(2):
        for k in range(n_z):
            at = pl.multiple_of(side * half + lax.rem(where[3] + k, n_z) * span, span)
            cols[pl.ds(at, span), :] = shards[side * n_z + k][...]
    cols_store.start()
    kept_all[:block, :] = scale_base2 * contract(rows[:block, :], cols[...], 1, 1)
    group_load.wait()
    row_groups, col_groups = group_rows(where, groups)
    ci = col_ids(where, n_cols, span)
    cg = jnp.concatenate(col_groups, axis=1)

    def fill(i):
        here = slice(i * block, (i + 1) * block)
        ri = row_ids(where, i * block, block, span)
        per = block // lanes
        rg = as_column(jnp.concatenate(row_groups[i * per : (i + 1) * per], axis=1))
        scores = scale_base2 * contract(rows[here, :], cols[...], 1, 1) if i else kept_all[here, :]
        valid = jnp.logical_or(rg != cg, ri == ci)
        kept_all[here, :] = jnp.where(valid, scores, floor_value)
        stores[i].start()

    peak = jnp.full((1, n_cols), floor_value, jnp.float32)
    total = jnp.zeros((1, n_cols), jnp.float32)
    fill(0)
    for i in range(n_blocks):
        if i + 1 < n_blocks:
            fill(i + 1)
        kept = kept_all[i * block : (i + 1) * block, :]
        row_peak = jnp.max(kept, axis=1, keepdims=True)
        row_total = jnp.sum(jnp.exp2(kept - row_peak), axis=1, keepdims=True)
        row_lse = fold(as_row(row_peak + jnp.log2(row_total)))
        for j in range(block // lanes):
            row_ref[:, i * block // lanes + j : i * block // lanes + j + 1, :] = jnp.broadcast_to(
                row_lse[None, j : j + 1, :], (row_ref.shape[0], 1, lanes)
            )
        top = jnp.maximum(peak, jnp.max(kept, axis=0, keepdims=True))
        total = total * jnp.exp2(peak - top) + jnp.sum(jnp.exp2(kept - top), axis=0, keepdims=True)
        peak = top
    col_lse = by_core(fold(peak + jnp.log2(total)), where[1])
    col_ref[...] = jnp.broadcast_to(col_lse[None], col_ref.shape)
    for copy in (cols_store, *stores):
        copy.wait()


def block_stats(rows, groups, shards, n_row, n_col):
    n_rows, width = rows.shape
    n_cols = len(shards) * shards[0].shape[0]
    return pl.pallas_call(
        stats_kernel,
        in_specs=[in_vmem, in_hbm] + [in_vmem] * len(shards),
        out_specs=[in_hbm, in_hbm, in_vmem, in_vmem],
        out_shape=[
            jax.ShapeDtypeStruct((n_rows, n_cols), jnp.float32),
            jax.ShapeDtypeStruct((n_cols, width), jnp.bfloat16),
            jax.ShapeDtypeStruct((n_row, n_rows // lanes, lanes), jnp.float32),
            jax.ShapeDtypeStruct((n_col, n_cols // lanes, lanes), jnp.float32),
        ],
        scratch_shapes=[
            pltpu.VMEM((n_rows, n_cols), jnp.float32),
            pltpu.VMEM((n_cols, width), jnp.bfloat16),
            pltpu.VMEM(groups.shape, groups.dtype),
            pltpu.SemaphoreType.DMA((n_rows // block + 2,)),
        ],
        compiler_params=params(55),
        cost_estimate=estimate(2 * n_rows * n_cols * width, 8, 2 * n_rows * n_cols),
        name="stats",
    )(rows, groups, *shards)


def merge(parts):
    top = parts[0]
    for part in parts[1:]:
        top = jnp.maximum(top, part)
    total = jnp.exp2(parts[0] - top)
    for part in parts[1:]:
        total = total + jnp.exp2(part - top)
    return top + jnp.log2(total)


def grad_kernel(kept_ref, cols_ref, row_parts, col_parts, col_others, image_ref, grad_ref, kept_all, cols, grads, image, sems):
    where = here_in_mesh()
    n_rows, n_cols = kept_ref.shape
    n_blocks = n_rows // block
    span = 64

    def piece(i):
        return pl.ds(i * block, block)

    kept_loads = [
        pltpu.make_async_copy(kept_ref.at[piece(i), :], kept_all.at[piece(i), :], sems.at[i]) for i in range(n_blocks)
    ]
    cols_load = pltpu.make_async_copy(cols_ref, cols, sems.at[n_blocks])
    image_stores = [
        pltpu.make_async_copy(image.at[piece(i), :], image_ref.at[piece(i), :], sems.at[n_blocks + 1 + i])
        for i in range(n_blocks)
    ]
    grad_stores = [
        pltpu.make_async_copy(grads.at[piece(i), :], grad_ref.at[piece(i), :], sems.at[2 * n_blocks + 1 + i])
        for i in range(n_blocks)
    ]
    for copy in (kept_loads[0], cols_load, *kept_loads[1:]):
        copy.start()
    ci = col_ids(where, n_cols, span)
    row_lse = merge([row_parts[i] for i in range(row_parts.shape[0])])
    col_lse = unfold(by_core(merge([ref[i] for ref in (col_parts, col_others) for i in range(ref.shape[0])]), where[1]))

    def fill(i):
        here = slice(i * block, (i + 1) * block)
        ri = row_ids(where, i * block, block, span)
        lse = as_column(unfold(row_lse[i * block // lanes : (i + 1) * block // lanes, :]))
        kept = kept_all[here, :]
        weight = jnp.exp2(kept - lse) + jnp.exp2(kept - col_lse)
        grad = 0.5 * weight - jnp.where(ri == ci, 1.0, 0.0)
        grads[here, :] = grad.astype(jnp.bfloat16)

    kept_loads[0].wait()
    fill(0)
    cols_load.wait()
    for i in range(n_blocks):
        if i + 1 < n_blocks:
            kept_loads[i + 1].wait()
            fill(i + 1)
        here = slice(i * block, (i + 1) * block)
        image[here, :] = contract(grads[here, :], cols[...], 1, 0).astype(jnp.bfloat16)
        image_stores[i].start()
        grad_stores[i].start()
    for copy in (*image_stores, *grad_stores):
        copy.wait()


def block_grad(kept, cols, row_parts, col_parts, col_others):
    n_rows, n_cols = kept.shape
    width = cols.shape[1]
    return pl.pallas_call(
        grad_kernel,
        in_specs=[in_hbm] * 2 + [in_vmem] * 3,
        out_specs=[in_hbm] * 2,
        out_shape=[
            jax.ShapeDtypeStruct((n_rows, width), jnp.bfloat16),
            jax.ShapeDtypeStruct((n_rows, n_cols), jnp.bfloat16),
        ],
        scratch_shapes=[
            pltpu.VMEM((n_rows, n_cols), jnp.float32),
            pltpu.VMEM((n_cols, width), jnp.bfloat16),
            pltpu.VMEM((n_rows, n_cols), jnp.bfloat16),
            pltpu.VMEM((n_rows, width), jnp.bfloat16),
            pltpu.SemaphoreType.DMA((3 * (n_rows // block) + 1,)),
        ],
        compiler_params=params(60),
        cost_estimate=estimate(2 * n_rows * n_cols * width, 12, 2 * n_rows * n_cols),
        name="grad",
    )(kept, cols, row_parts, col_parts, col_others)


def text_kernel(grad_ref, rows_ref, other_ref, other_rows_ref, own_ref, *refs):
    n_z = len(refs) - 3
    sent, (grads, rows, total, sems) = refs[: n_z - 1], refs[n_z - 1 :]
    n_cols = total.shape[0]
    span = n_cols // n_z
    depth = rows_ref.shape[0] // 2
    parts = [(i, j) for i in range(2) for j in range(2)]
    loads = {}
    for i, j in parts:
        here = pl.ds(j * depth, depth)
        pair = ((grad_ref, rows_ref), (other_ref, other_rows_ref))[i]
        loads[i, j] = [
            pltpu.make_async_copy(pair[0].at[here, pl.ds(i * n_cols, n_cols)], grads.at[i, here, :], sems.at[4 * i + 2 * j]),
            pltpu.make_async_copy(pair[1].at[here, :], rows.at[i, here, :], sems.at[4 * i + 2 * j + 1]),
        ]
        for copy in loads[i, j]:
            copy.start()
    for i, j in parts:
        for copy in loads[i, j]:
            copy.wait()
        deep = slice(j * depth, (j + 1) * depth)
        for at in range(0, n_cols, block):
            here = slice(at, at + block)
            part = contract(grads[i, deep, here], rows[i, deep, :], 0, 0)
            if i + j == 0:
                total[here, :] = part
            else:
                total[here, :] += part
    for k in range(n_z):
        at = pl.multiple_of(lax.rem(lax.axis_index("z") + k, n_z) * span, span)
        value = total[pl.ds(at, span), :]
        if k == 0:
            own_ref[...] = value
        else:
            sent[k - 1][...] = value.astype(jnp.bfloat16)


def text_terms(grad, rows, other, other_rows, n_z):
    n_rows, n_cols = grad.shape[0], grad.shape[1] // 2
    width = rows.shape[1]
    span = n_cols // n_z
    return pl.pallas_call(
        text_kernel,
        in_specs=[in_hbm] * 4,
        out_specs=[in_vmem] * n_z,
        out_shape=[jax.ShapeDtypeStruct((span, width), jnp.float32)]
        + [jax.ShapeDtypeStruct((span, width), jnp.bfloat16)] * (n_z - 1),
        scratch_shapes=[
            pltpu.VMEM((2, n_rows, n_cols), jnp.bfloat16),
            pltpu.VMEM((2, n_rows, width), jnp.bfloat16),
            pltpu.VMEM((n_cols, width), jnp.float32),
            pltpu.SemaphoreType.DMA((8,)),
        ],
        compiler_params=params(58),
        cost_estimate=estimate(4 * n_rows * n_cols * width, 8),
        name="text_terms",
    )(grad, rows, other, other_rows)


def sum_kernel(image_parts, own_ref, *refs):
    text_parts, (image_ref, text_ref, own, sem) = refs[:-4], refs[-4:]
    load = pltpu.make_async_copy(own_ref, own, sem)
    load.start()
    total = image_parts[0].astype(jnp.float32)
    for i in range(1, image_parts.shape[0]):
        total = total + image_parts[i].astype(jnp.float32)
    image_ref[...] = logit_scale * total
    total = text_parts[0][...].astype(jnp.float32)
    for ref in text_parts[1:]:
        total = total + ref[...].astype(jnp.float32)
    load.wait()
    total = total + own[...]
    text_ref[...] = logit_scale * total


def final_sums(image_parts, own, text_parts):
    n_plane, span, width = image_parts.shape
    return pl.pallas_call(
        sum_kernel,
        in_specs=[in_vmem, in_hbm] + [in_vmem] * len(text_parts),
        out_specs=[in_vmem] * 2,
        out_shape=[jax.ShapeDtypeStruct((span, width), jnp.float32)] * 2,
        scratch_shapes=[pltpu.VMEM((span, width), jnp.float32), pltpu.SemaphoreType.DMA],
        compiler_params=params(8),
        cost_estimate=estimate(span * width * 24, 4),
        name="sums",
    )(image_parts, own, *text_parts)


def per_device(image_emb, text_emb, caption_group):
    span, width = image_emb.shape
    n_y, n_core, n_x, n_z = (lax.axis_size(a) for a in axes)
    n_plane = n_y * n_x
    groups = caption_group.reshape(-1, lanes)

    rows = lax.all_to_all(repeat(image_emb, n_plane), plane, 0, 0)
    rows = rows.reshape(n_plane * span, width)
    shards = {0: text_emb}
    for k in range(1, n_z // 2):
        shards[n_z - k] = shift_z(shards[(n_z - k + 1) % n_z], 1)
        shards[k] = shift_z(shards[k - 1], -1)
    shards[n_z // 2] = shift_z(shards[n_z // 2 - 1], -1)
    near = [shards[k] for k in range(n_z)]
    far = [swap_core(shard) for shard in near]

    kept, cols, row_part, col_part = block_stats(rows, groups, near + far, n_plane, n_z)
    row_parts = lax.all_to_all(row_part, plane, 0, 0)
    col_parts = lax.all_to_all(col_part, "z", 0, 0)
    col_others = swap_core(col_parts)
    other_rows = swap_core(rows)

    image_part, grad = block_grad(kept, cols, row_parts, col_parts, col_others)
    image_parts = lax.all_to_all(image_part.reshape(n_plane, span, width), plane, 0, 0)
    own, *sent = text_terms(grad, rows, swap_core(grad), other_rows, n_z)
    text_parts = [shift_z(sent[k - 1], k) for k in z_steps(n_z)]
    return tuple(final_sums(image_parts, own, text_parts))


def solution(mesh):
    fine = Mesh(mesh.devices.reshape(4, 2, 4, 8), axes)
    return jax.shard_map(
        per_device,
        mesh=fine,
        in_specs=(P(axes, None), P(("x", "z", "y", "core"), None), P()),
        out_specs=(P(axes, None), P(("x", "z", "y", "core"), None)),
        check_vma=False,
    )
```

```python
import math

import jax
import jax.numpy as jnp
from jax import lax
from jax.experimental import pallas as pl
from jax.experimental.pallas import tpu as pltpu
from jax.sharding import Mesh, PartitionSpec as P

logit_scale = 100.0
scale_base2 = logit_scale / math.log(2.0)
floor_value = -1e30
mib = 1024 * 1024
lanes = 128
block = 256

axes = ("y", "core", "x", "z")
plane = ("y", "x")
in_vmem = pl.BlockSpec(memory_space=pltpu.VMEM)
in_hbm = pl.BlockSpec(memory_space=pltpu.HBM)


def swap_core(values):
    return lax.ppermute(values, "core", [(0, 1), (1, 0)])


def shift(values, axis, step):
    size = lax.axis_size(axis)
    return lax.ppermute(values, axis, [(i, (i + step) % size) for i in range(size)])


def shift_z(values, step):
    return shift(values, "z", step)


def z_steps(size):
    steps = [size // 2]
    for step in range(size // 2 - 1, 0, -1):
        steps += [step, size - step]
    return steps


def contract(a, b, dim_a, dim_b):
    return lax.dot_general(a, b, (((dim_a,), (dim_b,)), ((), ())), preferred_element_type=jnp.float32)


def as_column(row):
    return jnp.broadcast_to(row, (lanes, row.shape[1])).T[:, 0:1]


def as_row(column):
    return jnp.broadcast_to(column, (column.shape[0], lanes)).T[0:1, :]


def fold(row):
    return jnp.concatenate([row[:, i : i + lanes] for i in range(0, row.shape[1], lanes)], axis=0)


def unfold(tile):
    return jnp.concatenate([tile[i : i + 1, :] for i in range(tile.shape[0])], axis=1)


def by_core(tile, core):
    half = tile.shape[0] // 2
    return jnp.where(core == 0, tile, jnp.concatenate([tile[half:], tile[:half]], axis=0))


def estimate(flops, megabytes, exps=0):
    return pl.CostEstimate(flops=flops, bytes_accessed=megabytes * mib, transcendentals=exps)


def params(megabytes):
    return pltpu.CompilerParams(vmem_limit_bytes=int(megabytes * mib))


def here_in_mesh():
    return [lax.axis_index(name) for name in axes]


def row_ids(place, start, count, span):
    y, core, x, z = place
    at = start + lax.broadcasted_iota(jnp.int32, (count, 1), 0)
    member = at // span
    n_x, n_z, n_core = 4, 8, 2
    return (((member // n_x * n_core + core) * n_x + member % n_x) * n_z + z) * span + at % span


def col_ids(place, count, span):
    y, core, x, z = place
    n_y, n_z, n_core = 4, 8, 2
    at = lax.broadcasted_iota(jnp.int32, (1, count), 1)
    part = at // span
    side = jnp.where(part < n_z, core, 1 - core)
    return (((x * n_z + part % n_z) * n_y + y) * n_core + side) * span + at % span


def halves(a, b, which):
    low = lax.broadcasted_iota(jnp.int32, a.shape, 1) < lanes // 2
    turned_a = jnp.where(which == 0, a, pltpu.roll(a, lanes // 2, 1))
    turned_b = jnp.where(which == 0, pltpu.roll(b, lanes // 2, 1), b)
    return jnp.where(low, turned_a, turned_b)


def group_rows(place, group_ref):
    y, core, x, z = place
    n_x, n_z, n_plane = 4, 8, 16

    def ids(at):
        return group_ref[pl.ds(at, 1), :].astype(jnp.float32)

    rows = []
    for j in range(n_plane // 2):
        a, b = [ids(((m // n_x) * 2 + core) * 16 + (m % n_x) * 4 + z // 2) for m in (2 * j, 2 * j + 1)]
        rows.append(halves(a, b, lax.rem(z, 2)))
    cols = []
    for side in (core, 1 - core):
        for j in range(n_z // 2):
            a, b = [ids((x * n_z + m) * 4 + y) for m in (2 * j, 2 * j + 1)]
            cols.append(halves(a, b, side))
    return rows, cols


def repeat_kernel(in_ref, out_ref, held, sems):
    load = pltpu.make_async_copy(in_ref, held, sems.at[0])
    load.start()
    load.wait()
    copies = [pltpu.make_async_copy(held, out_ref.at[i], sems.at[1 + i]) for i in range(out_ref.shape[0])]
    for copy in copies:
        copy.start()
    for copy in copies:
        copy.wait()


def repeat(values, count):
    return pl.pallas_call(
        repeat_kernel,
        in_specs=[in_hbm],
        out_specs=in_hbm,
        out_shape=jax.ShapeDtypeStruct((count,) + values.shape, values.dtype),
        scratch_shapes=[pltpu.VMEM(values.shape, values.dtype), pltpu.SemaphoreType.DMA((1 + count,))],
        compiler_params=params(60),
        cost_estimate=estimate(0, 2),
        name="repeat",
    )(values)


def stats_kernel(rows, group_ref, *refs):
    shards, (near_ref, far_ref, cols_ref, rows_ref, row_ref, col_ref, kept_all, cols, groups, sems) = refs[:-10], refs[-10:]
    where = here_in_mesh()
    n_rows, n_cols = kept_all.shape
    half = n_cols // 2
    n_blocks = n_rows // block
    n_z = len(shards) // 2
    span = half // n_z

    stores = []
    for i in range(n_blocks):
        for side, ref in enumerate((near_ref, far_ref)):
            here = pl.ds(i * block, block)
            there = pl.ds(side * half, half)
            stores.append(pltpu.make_async_copy(kept_all.at[here, there], ref.at[here, :], sems.at[2 * i + side]))
    cols_store = pltpu.make_async_copy(cols, cols_ref, sems.at[2 * n_blocks])
    group_load = pltpu.make_async_copy(group_ref, groups, sems.at[2 * n_blocks + 1])
    group_load.start()
    rows_store = pltpu.make_async_copy(rows, rows_ref, sems.at[2 * n_blocks + 2])
    for side in range(2):
        for k in range(n_z):
            at = pl.multiple_of(side * half + lax.rem(where[3] + k, n_z) * span, span)
            cols[pl.ds(at, span), :] = shards[side * n_z + k][...]
    cols_store.start()
    rows_store.start()
    kept_all[:block, :] = scale_base2 * contract(rows[:block, :], cols[...], 1, 1)
    group_load.wait()
    row_groups, col_groups = group_rows(where, groups)
    ci = col_ids(where, n_cols, span)
    cg = jnp.concatenate(col_groups, axis=1)

    def fill(i):
        here = slice(i * block, (i + 1) * block)
        ri = row_ids(where, i * block, block, span)
        per = block // lanes
        rg = as_column(jnp.concatenate(row_groups[i * per : (i + 1) * per], axis=1))
        scores = scale_base2 * contract(rows[here, :], cols[...], 1, 1) if i else kept_all[here, :]
        valid = jnp.logical_or(rg != cg, ri == ci)
        kept_all[here, :] = jnp.where(valid, scores, floor_value)
        stores[2 * i].start()
        stores[2 * i + 1].start()

    peak = jnp.full((1, n_cols), floor_value, jnp.float32)
    total = jnp.zeros((1, n_cols), jnp.float32)
    fill(0)
    for i in range(n_blocks):
        if i + 1 < n_blocks:
            fill(i + 1)
        kept = kept_all[i * block : (i + 1) * block, :]
        row_peak = jnp.max(kept, axis=1, keepdims=True)
        row_total = jnp.sum(jnp.exp2(kept - row_peak), axis=1, keepdims=True)
        row_lse = fold(as_row(row_peak + jnp.log2(row_total)))
        for j in range(block // lanes):
            row_ref[i * block // lanes + j : i * block // lanes + j + 1, :] = row_lse[j : j + 1, :]
        top = jnp.maximum(peak, jnp.max(kept, axis=0, keepdims=True))
        total = total * jnp.exp2(peak - top) + jnp.sum(jnp.exp2(kept - top), axis=0, keepdims=True)
        peak = top
    col_lse = by_core(fold(peak + jnp.log2(total)), where[1])
    col_ref[...] = jnp.broadcast_to(col_lse[None], col_ref.shape)
    for copy in (cols_store, rows_store, *stores):
        copy.wait()


def block_stats(rows, groups, shards, n_col):
    n_rows, width = rows.shape
    n_cols = len(shards) * shards[0].shape[0]
    return pl.pallas_call(
        stats_kernel,
        in_specs=[in_vmem, in_hbm] + [in_vmem] * len(shards),
        out_specs=[in_hbm, in_hbm, in_hbm, in_hbm, in_vmem, in_vmem],
        out_shape=[
            jax.ShapeDtypeStruct((n_rows, n_cols // 2), jnp.float32),
            jax.ShapeDtypeStruct((n_rows, n_cols // 2), jnp.float32),
            jax.ShapeDtypeStruct((n_cols, width), jnp.bfloat16),
            jax.ShapeDtypeStruct((n_rows, width), jnp.bfloat16),
            jax.ShapeDtypeStruct((n_rows // lanes, lanes), jnp.float32),
            jax.ShapeDtypeStruct((n_col, n_cols // lanes, lanes), jnp.float32),
        ],
        scratch_shapes=[
            pltpu.VMEM((n_rows, n_cols), jnp.float32),
            pltpu.VMEM((n_cols, width), jnp.bfloat16),
            pltpu.VMEM(groups.shape, groups.dtype),
            pltpu.SemaphoreType.DMA((2 * (n_rows // block) + 3,)),
        ],
        compiler_params=params(50),
        cost_estimate=estimate(2 * n_rows * n_cols * width, 8, 2 * n_rows * n_cols),
        name="stats",
    )(rows, groups, *shards)


def merge(parts):
    top = parts[0]
    for part in parts[1:]:
        top = jnp.maximum(top, part)
    total = jnp.exp2(parts[0] - top)
    for part in parts[1:]:
        total = total + jnp.exp2(part - top)
    return top + jnp.log2(total)


def grad_kernel(near_ref, far_ref, other_ref, cols_ref, rows_ref, other_rows_ref, row_parts, col_parts, col_others, image_ref, own_ref, *refs):
    sent, (kept, other, cols, rows, grads, other_grads, image, total, sems) = refs[:-9], refs[-9:]
    y, core, x, z = here_in_mesh()
    n_rows, n_cols = kept.shape
    half = n_cols // 2
    n_blocks = n_rows // block
    n_z = len(sent) + 1
    span = half // n_z
    per = block // lanes

    def piece(i):
        return pl.ds(i * block, block)

    loads = []
    for i in range(n_blocks):
        for side, ref in enumerate((near_ref, far_ref)):
            there = kept.at[piece(i), pl.ds(side * half, half)]
            loads.append(pltpu.make_async_copy(ref.at[piece(i), :], there, sems.at[2 * i + side]))
    at = 2 * n_blocks
    cols_load = pltpu.make_async_copy(cols_ref, cols, sems.at[at])
    other_load = pltpu.make_async_copy(other_ref, other, sems.at[at + 1])
    rows_load = pltpu.make_async_copy(rows_ref, rows.at[0], sems.at[at + 2])
    other_rows_load = pltpu.make_async_copy(other_rows_ref, rows.at[1], sems.at[at + 3])
    image_stores = [
        pltpu.make_async_copy(image.at[piece(i), :], image_ref.at[piece(i), :], sems.at[at + 4 + i])
        for i in range(n_blocks)
    ]
    for copy in (*loads[:2], cols_load, *loads[2:], rows_load, other_load, other_rows_load):
        copy.start()
    ci = col_ids((y, core, x, z), n_cols, span)
    row_lse = merge([row_parts[i, 0] for i in range(row_parts.shape[0])])
    other_lse = merge([row_parts[i, 1] for i in range(row_parts.shape[0])])
    col_lse = merge([ref[i] for ref in (col_parts, col_others) for i in range(ref.shape[0])])
    col_lse = unfold(by_core(col_lse, core))

    def gradient(logits, i, side, lse_tile, ci, col_lse):
        ri = row_ids((y, side, x, z), i * block, block, span)
        lse = as_column(unfold(lse_tile[i * per : (i + 1) * per, :]))
        weight = jnp.exp2(logits - lse) + jnp.exp2(logits - col_lse)
        grad = 0.5 * weight - jnp.where(ri == ci, 1.0, 0.0)
        return grad.astype(jnp.bfloat16)

    def fill(i):
        here = slice(i * block, (i + 1) * block)
        grads[here, :] = gradient(kept[here, :], i, core, row_lse, ci, col_lse)

    def fill_other(i):
        here = slice(i * block, (i + 1) * block)
        other_grads[here, :] = gradient(other[here, :], i, 1 - core, other_lse, ci[:, :half], col_lse[:, :half])

    loads[0].wait()
    loads[1].wait()
    fill(0)
    cols_load.wait()
    for i in range(n_blocks):
        if i + 1 < n_blocks:
            loads[2 * i + 2].wait()
            loads[2 * i + 3].wait()
            fill(i + 1)
        here = slice(i * block, (i + 1) * block)
        image[here, :] = contract(grads[here, :], cols[...], 1, 0).astype(jnp.bfloat16)
        image_stores[i].start()
    rows_load.wait()
    other_load.wait()
    for i in range(n_blocks):
        fill_other(i)
    for i in range(0, half, block):
        here = slice(i, i + block)
        total[here, :] = contract(grads[:, here], rows[0], 0, 0)
    other_rows_load.wait()
    for i in range(0, half, block):
        here = slice(i, i + block)
        total[here, :] += contract(other_grads[:, here], rows[1], 0, 0)
    for k in range(n_z):
        value = total[pl.ds(pl.multiple_of(lax.rem(z + k, n_z) * span, span), span), :]
        if k == 0:
            own_ref[...] = value
        else:
            sent[k - 1][...] = value.astype(jnp.bfloat16)
    for copy in image_stores:
        copy.wait()


def block_grad(near, far, other, cols, rows, other_rows, parts, n_z):
    n_rows, width = rows.shape
    half = near.shape[1]
    n_cols = 2 * half
    shard = (half // n_z, width)
    return pl.pallas_call(
        grad_kernel,
        in_specs=[in_hbm] * 6 + [in_vmem] * len(parts),
        out_specs=[in_hbm] + [in_vmem] * n_z,
        out_shape=[
            jax.ShapeDtypeStruct((n_rows, width), jnp.bfloat16),
            jax.ShapeDtypeStruct(shard, jnp.float32),
        ]
        + [jax.ShapeDtypeStruct(shard, jnp.bfloat16)] * (n_z - 1),
        scratch_shapes=[
            pltpu.VMEM((n_rows, n_cols), jnp.float32),
            pltpu.VMEM((n_rows, half), jnp.float32),
            pltpu.VMEM((n_cols, width), jnp.bfloat16),
            pltpu.VMEM((2, n_rows, width), jnp.bfloat16),
            pltpu.VMEM((n_rows, n_cols), jnp.bfloat16),
            pltpu.VMEM((n_rows, half), jnp.bfloat16),
            pltpu.VMEM((n_rows, width), jnp.bfloat16),
            pltpu.VMEM((half, width), jnp.float32),
            pltpu.SemaphoreType.DMA((3 * (n_rows // block) + 4,)),
        ],
        compiler_params=params(53.5),
        cost_estimate=estimate(4 * n_rows * n_cols * width, 14, 3 * n_rows * n_cols),
        name="grad",
    )(near, far, other, cols, rows, other_rows, *parts)


def sum_kernel(image_parts, own_ref, *refs):
    text_parts, (image_ref, text_ref, own, sem) = refs[:-4], refs[-4:]
    load = pltpu.make_async_copy(own_ref, own, sem)
    load.start()
    total = image_parts[0].astype(jnp.float32)
    for i in range(1, image_parts.shape[0]):
        total = total + image_parts[i].astype(jnp.float32)
    image_ref[...] = logit_scale * total
    total = text_parts[0][...].astype(jnp.float32)
    for ref in text_parts[1:]:
        total = total + ref[...].astype(jnp.float32)
    load.wait()
    total = total + own[...]
    text_ref[...] = logit_scale * total


def final_sums(image_parts, own, text_parts):
    n_plane, span, width = image_parts.shape
    return pl.pallas_call(
        sum_kernel,
        in_specs=[in_vmem, in_hbm] + [in_vmem] * len(text_parts),
        out_specs=[in_vmem] * 2,
        out_shape=[jax.ShapeDtypeStruct((span, width), jnp.float32)] * 2,
        scratch_shapes=[pltpu.VMEM((span, width), jnp.float32), pltpu.SemaphoreType.DMA],
        compiler_params=params(8),
        cost_estimate=estimate(span * width * 24, 4),
        name="sums",
    )(image_parts, own, *text_parts)


def per_device(image_emb, text_emb, caption_group):
    span, width = image_emb.shape
    n_y, n_core, n_x, n_z = (lax.axis_size(a) for a in axes)
    n_plane = n_y * n_x
    groups = caption_group.reshape(-1, lanes)

    rows = lax.all_to_all(repeat(image_emb, n_plane), plane, 0, 0)
    rows = rows.reshape(n_plane * span, width)
    shards = {0: text_emb}
    for k in range(1, n_z // 2):
        shards[n_z - k] = shift_z(shards[(n_z - k + 1) % n_z], 1)
        shards[k] = shift_z(shards[k - 1], -1)
    shards[n_z // 2] = shift_z(shards[n_z // 2 - 1], -1)
    near = [shards[k] for k in range(n_z)]
    far = [swap_core(shard) for shard in near]

    near_kept, far_kept, cols, rows, row_part, col_part = block_stats(rows, groups, near + far, n_z)
    pair = jnp.stack([row_part, swap_core(row_part)])
    col_parts = lax.all_to_all(col_part, "z", 0, 0)
    row_parts = lax.all_to_all(jnp.broadcast_to(pair[None], (n_plane,) + pair.shape), plane, 0, 0)
    other_kept = swap_core(far_kept)
    other_rows = swap_core(rows)
    parts = [row_parts, col_parts, swap_core(col_parts)]

    image_part, own, *sent = block_grad(near_kept, far_kept, other_kept, cols, rows, other_rows, parts, n_z)
    image_parts = lax.all_to_all(image_part.reshape(n_plane, span, width), plane, 0, 0)
    text_parts = [shift_z(sent[k - 1], k) for k in z_steps(n_z)]
    return tuple(final_sums(image_parts, own, text_parts))


def solution(mesh):
    fine = Mesh(mesh.devices.reshape(4, 2, 4, 8), axes)
    return jax.shard_map(
        per_device,
        mesh=fine,
        in_specs=(P(axes, None), P(("x", "z", "y", "core"), None), P()),
        out_specs=(P(axes, None), P(("x", "z", "y", "core"), None)),
        check_vma=False,
    )
```

```python
import math

import jax
import jax.numpy as jnp
from jax import lax
from jax.experimental import pallas as pl
from jax.experimental.pallas import tpu as pltpu
from jax.sharding import Mesh, PartitionSpec as P

logit_scale = 100.0
scale_base2 = logit_scale / math.log(2.0)
floor_value = -1e30
mib = 1024 * 1024
lanes = 128
block = 256

axes = ("y", "core", "x", "z")
plane = ("y", "x")
in_vmem = pl.BlockSpec(memory_space=pltpu.VMEM)
in_hbm = pl.BlockSpec(memory_space=pltpu.HBM)


def swap_core(values):
    return lax.ppermute(values, "core", [(0, 1), (1, 0)])


def shift(values, axis, step):
    size = lax.axis_size(axis)
    return lax.ppermute(values, axis, [(i, (i + step) % size) for i in range(size)])


def shift_z(values, step):
    return shift(values, "z", step)


def z_steps(size):
    steps = [size // 2]
    for step in range(size // 2 - 1, 0, -1):
        steps += [step, size - step]
    return steps


def contract(a, b, dim_a, dim_b):
    return lax.dot_general(a, b, (((dim_a,), (dim_b,)), ((), ())), preferred_element_type=jnp.float32)


def as_column(row):
    return jnp.broadcast_to(row, (lanes, row.shape[1])).T[:, 0:1]


def as_row(column):
    return jnp.broadcast_to(column, (column.shape[0], lanes)).T[0:1, :]


def fold(row):
    return jnp.concatenate([row[:, i : i + lanes] for i in range(0, row.shape[1], lanes)], axis=0)


def unfold(tile):
    return jnp.concatenate([tile[i : i + 1, :] for i in range(tile.shape[0])], axis=1)


def by_core(tile, core):
    half = tile.shape[0] // 2
    return jnp.where(core == 0, tile, jnp.concatenate([tile[half:], tile[:half]], axis=0))


def estimate(flops, megabytes, exps=0):
    return pl.CostEstimate(flops=flops, bytes_accessed=megabytes * mib, transcendentals=exps)


def params(megabytes):
    return pltpu.CompilerParams(vmem_limit_bytes=int(megabytes * mib))


def here_in_mesh():
    return [lax.axis_index(name) for name in axes]


def row_ids(place, start, count, span):
    y, core, x, z = place
    at = start + lax.broadcasted_iota(jnp.int32, (count, 1), 0)
    member = at // span
    n_x, n_z, n_core = 4, 8, 2
    return (((member // n_x * n_core + core) * n_x + member % n_x) * n_z + z) * span + at % span


def col_ids(place, count, span):
    y, core, x, z = place
    n_y, n_z, n_core = 4, 8, 2
    at = lax.broadcasted_iota(jnp.int32, (1, count), 1)
    part = at // span
    side = jnp.where(part < n_z, core, 1 - core)
    return (((x * n_z + part % n_z) * n_y + y) * n_core + side) * span + at % span


def halves(a, b, which):
    low = lax.broadcasted_iota(jnp.int32, a.shape, 1) < lanes // 2
    turned_a = jnp.where(which == 0, a, pltpu.roll(a, lanes // 2, 1))
    turned_b = jnp.where(which == 0, pltpu.roll(b, lanes // 2, 1), b)
    return jnp.where(low, turned_a, turned_b)


def group_rows(place, group_ref):
    y, core, x, z = place
    n_x, n_z, n_plane = 4, 8, 16

    def ids(at):
        return group_ref[pl.ds(at, 1), :].astype(jnp.float32)

    rows = []
    for j in range(n_plane // 2):
        a, b = [ids(((m // n_x) * 2 + core) * 16 + (m % n_x) * 4 + z // 2) for m in (2 * j, 2 * j + 1)]
        rows.append(halves(a, b, lax.rem(z, 2)))
    cols = []
    for side in (core, 1 - core):
        for j in range(n_z // 2):
            a, b = [ids((x * n_z + m) * 4 + y) for m in (2 * j, 2 * j + 1)]
            cols.append(halves(a, b, side))
    return rows, cols


def repeat_kernel(in_ref, out_ref, held, sems):
    load = pltpu.make_async_copy(in_ref, held, sems.at[0])
    load.start()
    load.wait()
    copies = [pltpu.make_async_copy(held, out_ref.at[i], sems.at[1 + i]) for i in range(out_ref.shape[0])]
    for copy in copies:
        copy.start()
    for copy in copies:
        copy.wait()


def repeat(values, count):
    return pl.pallas_call(
        repeat_kernel,
        in_specs=[in_hbm],
        out_specs=in_hbm,
        out_shape=jax.ShapeDtypeStruct((count,) + values.shape, values.dtype),
        scratch_shapes=[pltpu.VMEM(values.shape, values.dtype), pltpu.SemaphoreType.DMA((1 + count,))],
        compiler_params=params(60),
        cost_estimate=estimate(0, 2),
        name="repeat",
    )(values)


def stats_kernel(rows_ref, group_ref, *refs):
    shards, (near_ref, far_ref, cols_ref, row_ref, col_ref, kept_all, rows, cols, groups, sems) = refs[:-10], refs[-10:]
    where = here_in_mesh()
    n_rows, n_cols = kept_all.shape
    half = n_cols // 2
    n_blocks = n_rows // block
    n_z = len(shards) // 2
    span = half // n_z

    stores = []
    for i in range(n_blocks):
        for side, ref in enumerate((near_ref, far_ref)):
            here = pl.ds(i * block, block)
            there = pl.ds(side * half, half)
            stores.append(pltpu.make_async_copy(kept_all.at[here, there], ref.at[here, :], sems.at[2 * i + side]))
    cols_store = pltpu.make_async_copy(cols, cols_ref, sems.at[2 * n_blocks])
    group_load = pltpu.make_async_copy(group_ref, groups, sems.at[2 * n_blocks + 1])
    group_load.start()
    row_loads = []
    for i in range(n_blocks):
        here = pl.ds(i * block, block)
        row_loads.append(pltpu.make_async_copy(rows_ref.at[here, :], rows.at[here, :], sems.at[2 * n_blocks + 2 + i]))
        row_loads[i].start()
    for side in range(2):
        for k in range(n_z):
            at = pl.multiple_of(side * half + lax.rem(where[3] + k, n_z) * span, span)
            cols[pl.ds(at, span), :] = shards[side * n_z + k][...]
    cols_store.start()
    row_loads[0].wait()
    kept_all[:block, :] = scale_base2 * contract(rows[:block, :], cols[...], 1, 1)
    group_load.wait()
    for copy in row_loads[1:]:
        copy.wait()
    row_groups, col_groups = group_rows(where, groups)
    ci = col_ids(where, n_cols, span)
    cg = jnp.concatenate(col_groups, axis=1)

    def fill(i):
        here = slice(i * block, (i + 1) * block)
        ri = row_ids(where, i * block, block, span)
        per = block // lanes
        rg = as_column(jnp.concatenate(row_groups[i * per : (i + 1) * per], axis=1))
        scores = scale_base2 * contract(rows[here, :], cols[...], 1, 1) if i else kept_all[here, :]
        valid = jnp.logical_or(rg != cg, ri == ci)
        kept_all[here, :] = jnp.where(valid, scores, floor_value)
        stores[2 * i].start()
        stores[2 * i + 1].start()

    peak = jnp.full((1, n_cols), floor_value, jnp.float32)
    total = jnp.zeros((1, n_cols), jnp.float32)
    fill(0)
    for i in range(n_blocks):
        if i + 1 < n_blocks:
            fill(i + 1)
        kept = kept_all[i * block : (i + 1) * block, :]
        row_peak = jnp.max(kept, axis=1, keepdims=True)
        row_total = jnp.sum(jnp.exp2(kept - row_peak), axis=1, keepdims=True)
        row_lse = fold(as_row(row_peak + jnp.log2(row_total)))
        for j in range(block // lanes):
            row_ref[i * block // lanes + j : i * block // lanes + j + 1, :] = row_lse[j : j + 1, :]
        top = jnp.maximum(peak, jnp.max(kept, axis=0, keepdims=True))
        total = total * jnp.exp2(peak - top) + jnp.sum(jnp.exp2(kept - top), axis=0, keepdims=True)
        peak = top
    col_lse = by_core(fold(peak + jnp.log2(total)), where[1])
    col_ref[...] = jnp.broadcast_to(col_lse[None], col_ref.shape)
    for copy in (cols_store, *stores):
        copy.wait()


def block_stats(rows, groups, shards, n_col):
    n_rows, width = rows.shape
    n_cols = len(shards) * shards[0].shape[0]
    return pl.pallas_call(
        stats_kernel,
        in_specs=[in_hbm] * 2 + [in_vmem] * len(shards),
        out_specs=[in_hbm, in_hbm, in_hbm, in_vmem, in_vmem],
        out_shape=[
            jax.ShapeDtypeStruct((n_rows, n_cols // 2), jnp.float32),
            jax.ShapeDtypeStruct((n_rows, n_cols // 2), jnp.float32),
            jax.ShapeDtypeStruct((n_cols, width), jnp.bfloat16),
            jax.ShapeDtypeStruct((n_rows // lanes, lanes), jnp.float32),
            jax.ShapeDtypeStruct((n_col, n_cols // lanes, lanes), jnp.float32),
        ],
        scratch_shapes=[
            pltpu.VMEM((n_rows, n_cols), jnp.float32),
            pltpu.VMEM((n_rows, width), jnp.bfloat16),
            pltpu.VMEM((n_cols, width), jnp.bfloat16),
            pltpu.VMEM(groups.shape, groups.dtype),
            pltpu.SemaphoreType.DMA((3 * (n_rows // block) + 2,)),
        ],
        compiler_params=params(50),
        cost_estimate=estimate(2 * n_rows * n_cols * width, 8, 2 * n_rows * n_cols),
        name="stats",
    )(rows, groups, *shards)


def merge(parts):
    top = parts[0]
    for part in parts[1:]:
        top = jnp.maximum(top, part)
    total = jnp.exp2(parts[0] - top)
    for part in parts[1:]:
        total = total + jnp.exp2(part - top)
    return top + jnp.log2(total)


def grad_kernel(near_ref, far_ref, other_ref, cols_ref, rows_ref, other_rows_ref, row_parts, col_parts, col_others, image_ref, own_ref, *refs):
    sent, (kept, other, cols, rows, grads, other_grads, image, total, sems) = refs[:-9], refs[-9:]
    y, core, x, z = here_in_mesh()
    n_rows, n_cols = kept.shape
    half = n_cols // 2
    n_blocks = n_rows // block
    n_z = len(sent) + 1
    span = half // n_z
    per = block // lanes

    def piece(i):
        return pl.ds(i * block, block)

    loads = []
    for i in range(n_blocks):
        for side, ref in enumerate((near_ref, far_ref)):
            there = kept.at[piece(i), pl.ds(side * half, half)]
            loads.append(pltpu.make_async_copy(ref.at[piece(i), :], there, sems.at[2 * i + side]))
    at = 2 * n_blocks
    cols_load = pltpu.make_async_copy(cols_ref, cols, sems.at[at])
    other_load = pltpu.make_async_copy(other_ref, other, sems.at[at + 1])
    rows_load = pltpu.make_async_copy(rows_ref, rows.at[0], sems.at[at + 2])
    other_rows_load = pltpu.make_async_copy(other_rows_ref, rows.at[1], sems.at[at + 3])
    image_stores = [
        pltpu.make_async_copy(image.at[piece(i), :], image_ref.at[piece(i), :], sems.at[at + 4 + i])
        for i in range(n_blocks)
    ]
    for copy in (*loads[:2], cols_load, *loads[2:], rows_load, other_load, other_rows_load):
        copy.start()
    ci = col_ids((y, core, x, z), n_cols, span)
    row_lse = merge([row_parts[i, 0] for i in range(row_parts.shape[0])])
    other_lse = merge([row_parts[i, 1] for i in range(row_parts.shape[0])])
    col_lse = merge([ref[i] for ref in (col_parts, col_others) for i in range(ref.shape[0])])
    col_lse = unfold(by_core(col_lse, core))

    def gradient(logits, i, side, lse_tile, ci, col_lse):
        ri = row_ids((y, side, x, z), i * block, block, span)
        lse = as_column(unfold(lse_tile[i * per : (i + 1) * per, :]))
        weight = jnp.exp2(logits - lse) + jnp.exp2(logits - col_lse)
        grad = 0.5 * weight - jnp.where(ri == ci, 1.0, 0.0)
        return grad.astype(jnp.bfloat16)

    def fill(i):
        here = slice(i * block, (i + 1) * block)
        grads[here, :] = gradient(kept[here, :], i, core, row_lse, ci, col_lse)

    def fill_other(i):
        here = slice(i * block, (i + 1) * block)
        other_grads[here, :] = gradient(other[here, :], i, 1 - core, other_lse, ci[:, :half], col_lse[:, :half])

    loads[0].wait()
    loads[1].wait()
    fill(0)
    cols_load.wait()
    for i in range(n_blocks):
        if i + 1 < n_blocks:
            loads[2 * i + 2].wait()
            loads[2 * i + 3].wait()
            fill(i + 1)
        here = slice(i * block, (i + 1) * block)
        image[here, :] = contract(grads[here, :], cols[...], 1, 0).astype(jnp.bfloat16)
        image_stores[i].start()
    rows_load.wait()
    other_load.wait()
    for i in range(n_blocks):
        fill_other(i)
    for i in range(0, half, block):
        here = slice(i, i + block)
        total[here, :] = contract(grads[:, here], rows[0], 0, 0)
    other_rows_load.wait()
    for i in range(0, half, block):
        here = slice(i, i + block)
        total[here, :] += contract(other_grads[:, here], rows[1], 0, 0)
    for k in range(n_z):
        value = total[pl.ds(pl.multiple_of(lax.rem(z + k, n_z) * span, span), span), :]
        if k == 0:
            own_ref[...] = value
        else:
            sent[k - 1][...] = value.astype(jnp.bfloat16)
    for copy in image_stores:
        copy.wait()


def block_grad(near, far, other, cols, rows, other_rows, parts, n_z):
    n_rows, width = rows.shape
    half = near.shape[1]
    n_cols = 2 * half
    shard = (half // n_z, width)
    return pl.pallas_call(
        grad_kernel,
        in_specs=[in_hbm] * 6 + [in_vmem] * len(parts),
        out_specs=[in_hbm] + [in_vmem] * n_z,
        out_shape=[
            jax.ShapeDtypeStruct((n_rows, width), jnp.bfloat16),
            jax.ShapeDtypeStruct(shard, jnp.float32),
        ]
        + [jax.ShapeDtypeStruct(shard, jnp.bfloat16)] * (n_z - 1),
        scratch_shapes=[
            pltpu.VMEM((n_rows, n_cols), jnp.float32),
            pltpu.VMEM((n_rows, half), jnp.float32),
            pltpu.VMEM((n_cols, width), jnp.bfloat16),
            pltpu.VMEM((2, n_rows, width), jnp.bfloat16),
            pltpu.VMEM((n_rows, n_cols), jnp.bfloat16),
            pltpu.VMEM((n_rows, half), jnp.bfloat16),
            pltpu.VMEM((n_rows, width), jnp.bfloat16),
            pltpu.VMEM((half, width), jnp.float32),
            pltpu.SemaphoreType.DMA((3 * (n_rows // block) + 4,)),
        ],
        compiler_params=params(52),
        cost_estimate=estimate(4 * n_rows * n_cols * width, 14, 3 * n_rows * n_cols),
        name="grad",
    )(near, far, other, cols, rows, other_rows, *parts)


def sum_kernel(image_parts, own_ref, *refs):
    text_parts, (image_ref, text_ref, own, sem) = refs[:-4], refs[-4:]
    load = pltpu.make_async_copy(own_ref, own, sem)
    load.start()
    total = image_parts[0].astype(jnp.float32)
    for i in range(1, image_parts.shape[0]):
        total = total + image_parts[i].astype(jnp.float32)
    image_ref[...] = logit_scale * total
    total = text_parts[0][...].astype(jnp.float32)
    for ref in text_parts[1:]:
        total = total + ref[...].astype(jnp.float32)
    load.wait()
    total = total + own[...]
    text_ref[...] = logit_scale * total


def final_sums(image_parts, own, text_parts):
    n_plane, span, width = image_parts.shape
    return pl.pallas_call(
        sum_kernel,
        in_specs=[in_vmem, in_hbm] + [in_vmem] * len(text_parts),
        out_specs=[in_vmem] * 2,
        out_shape=[jax.ShapeDtypeStruct((span, width), jnp.float32)] * 2,
        scratch_shapes=[pltpu.VMEM((span, width), jnp.float32), pltpu.SemaphoreType.DMA],
        compiler_params=params(8),
        cost_estimate=estimate(span * width * 24, 4),
        name="sums",
    )(image_parts, own, *text_parts)


def per_device(image_emb, text_emb, caption_group):
    span, width = image_emb.shape
    n_y, n_core, n_x, n_z = (lax.axis_size(a) for a in axes)
    n_plane = n_y * n_x
    groups = caption_group.reshape(-1, lanes)

    rows = lax.all_to_all(repeat(image_emb, n_plane), plane, 0, 0)
    rows = rows.reshape(n_plane * span, width)
    shards = {0: text_emb}
    for k in range(1, n_z // 2):
        shards[n_z - k] = shift_z(shards[(n_z - k + 1) % n_z], 1)
        shards[k] = shift_z(shards[k - 1], -1)
    shards[n_z // 2] = shift_z(shards[n_z // 2 - 1], -1)
    near = [shards[k] for k in range(n_z)]
    far = [swap_core(shard) for shard in near]

    near_kept, far_kept, cols, row_part, col_part = block_stats(rows, groups, near + far, n_z)
    pair = jnp.stack([row_part, swap_core(row_part)])
    col_parts = lax.all_to_all(col_part, "z", 0, 0)
    row_parts = lax.all_to_all(jnp.broadcast_to(pair[None], (n_plane,) + pair.shape), plane, 0, 0)
    other_kept = swap_core(far_kept)
    other_rows = swap_core(rows)
    parts = [row_parts, col_parts, swap_core(col_parts)]

    image_part, own, *sent = block_grad(near_kept, far_kept, other_kept, cols, rows, other_rows, parts, n_z)
    image_parts = lax.all_to_all(image_part.reshape(n_plane, span, width), plane, 0, 0)
    text_parts = [shift_z(sent[k - 1], k) for k in z_steps(n_z)]
    return tuple(final_sums(image_parts, own, text_parts))


def solution(mesh):
    fine = Mesh(mesh.devices.reshape(4, 2, 4, 8), axes)
    return jax.shard_map(
        per_device,
        mesh=fine,
        in_specs=(P(axes, None), P(("x", "z", "y", "core"), None), P()),
        out_specs=(P(axes, None), P(("x", "z", "y", "core"), None)),
        check_vma=False,
    )
```

```python
import math

import jax
import jax.numpy as jnp
from jax import lax
from jax.experimental import pallas as pl
from jax.experimental.pallas import tpu as pltpu
from jax.sharding import Mesh, PartitionSpec as P

logit_scale = 100.0
scale_base2 = logit_scale / math.log(2.0)
floor_value = -1e30
mib = 1024 * 1024
lanes = 128
block = 256

axes = ("y", "core", "x", "z")
plane = ("x", "y")
in_vmem = pl.BlockSpec(memory_space=pltpu.VMEM)
in_hbm = pl.BlockSpec(memory_space=pltpu.HBM)


def swap_core(values):
    return lax.ppermute(values, "core", [(0, 1), (1, 0)])


def shift(values, axis, step):
    size = lax.axis_size(axis)
    return lax.ppermute(values, axis, [(i, (i + step) % size) for i in range(size)])


def shift_z(values, step):
    return shift(values, "z", step)


def z_steps(size):
    steps = [size // 2]
    for step in range(size // 2 - 1, 0, -1):
        steps += [step, size - step]
    return steps


def contract(a, b, dim_a, dim_b):
    return lax.dot_general(a, b, (((dim_a,), (dim_b,)), ((), ())), preferred_element_type=jnp.float32)


def as_column(row):
    return jnp.broadcast_to(row, (lanes, row.shape[1])).T[:, 0:1]


def as_row(column):
    return jnp.broadcast_to(column, (column.shape[0], lanes)).T[0:1, :]


def fold(row):
    return jnp.concatenate([row[:, i : i + lanes] for i in range(0, row.shape[1], lanes)], axis=0)


def unfold(tile):
    return jnp.concatenate([tile[i : i + 1, :] for i in range(tile.shape[0])], axis=1)


def by_core(tile, core):
    half = tile.shape[0] // 2
    return jnp.where(core == 0, tile, jnp.concatenate([tile[half:], tile[:half]], axis=0))


def estimate(flops, megabytes, exps=0):
    return pl.CostEstimate(flops=flops, bytes_accessed=megabytes * mib, transcendentals=exps)


def params(megabytes):
    return pltpu.CompilerParams(vmem_limit_bytes=int(megabytes * mib))


def here_in_mesh():
    return [lax.axis_index(name) for name in axes]


def row_ids(place, start, count, span):
    y, core, x, z = place
    at = start + lax.broadcasted_iota(jnp.int32, (count, 1), 0)
    member = at // span
    n_y, n_x, n_z, n_core = 4, 4, 8, 2
    return (((member % n_y * n_core + core) * n_x + member // n_y) * n_z + z) * span + at % span


def col_ids(place, count, span):
    y, core, x, z = place
    n_y, n_z, n_core = 4, 8, 2
    at = lax.broadcasted_iota(jnp.int32, (1, count), 1)
    part = at // span
    side = jnp.where(part < n_z, core, 1 - core)
    return (((x * n_z + part % n_z) * n_y + y) * n_core + side) * span + at % span


def halves(a, b, which):
    low = lax.broadcasted_iota(jnp.int32, a.shape, 1) < lanes // 2
    turned_a = jnp.where(which == 0, a, pltpu.roll(a, lanes // 2, 1))
    turned_b = jnp.where(which == 0, pltpu.roll(b, lanes // 2, 1), b)
    return jnp.where(low, turned_a, turned_b)


def group_rows(place, group_ref):
    y, core, x, z = place
    n_y, n_z, n_plane = 4, 8, 16

    def ids(at):
        return group_ref[pl.ds(at, 1), :].astype(jnp.float32)

    rows = []
    for j in range(n_plane // 2):
        a, b = [ids(((m % n_y) * 2 + core) * 16 + (m // n_y) * 4 + z // 2) for m in (2 * j, 2 * j + 1)]
        rows.append(halves(a, b, lax.rem(z, 2)))
    cols = []
    for side in (core, 1 - core):
        for j in range(n_z // 2):
            a, b = [ids((x * n_z + m) * 4 + y) for m in (2 * j, 2 * j + 1)]
            cols.append(halves(a, b, side))
    return rows, cols


def repeat_kernel(in_ref, out_ref, held, sems):
    load = pltpu.make_async_copy(in_ref, held, sems.at[0])
    load.start()
    load.wait()
    copies = [pltpu.make_async_copy(held, out_ref.at[i], sems.at[1 + i]) for i in range(out_ref.shape[0])]
    for copy in copies:
        copy.start()
    for copy in copies:
        copy.wait()


def repeat(values, count):
    return pl.pallas_call(
        repeat_kernel,
        in_specs=[in_hbm],
        out_specs=in_hbm,
        out_shape=jax.ShapeDtypeStruct((count,) + values.shape, values.dtype),
        scratch_shapes=[pltpu.VMEM(values.shape, values.dtype), pltpu.SemaphoreType.DMA((1 + count,))],
        compiler_params=params(60),
        cost_estimate=estimate(0, 2),
        name="repeat",
    )(values)


def stats_kernel(rows_ref, group_ref, *refs):
    shards, (near_ref, far_ref, cols_ref, row_ref, col_ref, kept_all, rows, cols, groups, sems) = refs[:-10], refs[-10:]
    where = here_in_mesh()
    n_rows, n_cols = kept_all.shape
    half = n_cols // 2
    n_blocks = n_rows // block
    n_z = len(shards) // 2
    span = half // n_z

    stores = []
    for i in range(n_blocks):
        for side, ref in enumerate((near_ref, far_ref)):
            here = pl.ds(i * block, block)
            there = pl.ds(side * half, half)
            stores.append(pltpu.make_async_copy(kept_all.at[here, there], ref.at[here, :], sems.at[2 * i + side]))
    cols_store = pltpu.make_async_copy(cols, cols_ref, sems.at[2 * n_blocks])
    group_load = pltpu.make_async_copy(group_ref, groups, sems.at[2 * n_blocks + 1])
    group_load.start()
    row_loads = []
    for i in range(n_blocks):
        here = pl.ds(i * block, block)
        row_loads.append(pltpu.make_async_copy(rows_ref.at[here, :], rows.at[here, :], sems.at[2 * n_blocks + 2 + i]))
        row_loads[i].start()
    for side in range(2):
        for k in range(n_z):
            at = pl.multiple_of(side * half + lax.rem(where[3] + k, n_z) * span, span)
            cols[pl.ds(at, span), :] = shards[side * n_z + k][...]
    cols_store.start()
    row_loads[0].wait()
    kept_all[:block, :] = scale_base2 * contract(rows[:block, :], cols[...], 1, 1)
    group_load.wait()
    for copy in row_loads[1:]:
        copy.wait()
    row_groups, col_groups = group_rows(where, groups)
    ci = col_ids(where, n_cols, span)
    cg = jnp.concatenate(col_groups, axis=1)

    def fill(i):
        here = slice(i * block, (i + 1) * block)
        ri = row_ids(where, i * block, block, span)
        per = block // lanes
        rg = as_column(jnp.concatenate(row_groups[i * per : (i + 1) * per], axis=1))
        scores = scale_base2 * contract(rows[here, :], cols[...], 1, 1) if i else kept_all[here, :]
        valid = jnp.logical_or(rg != cg, ri == ci)
        kept_all[here, :] = jnp.where(valid, scores, floor_value)
        stores[2 * i].start()
        stores[2 * i + 1].start()

    peak = jnp.full((1, n_cols), floor_value, jnp.float32)
    total = jnp.zeros((1, n_cols), jnp.float32)
    fill(0)
    for i in range(n_blocks):
        if i + 1 < n_blocks:
            fill(i + 1)
        kept = kept_all[i * block : (i + 1) * block, :]
        row_peak = jnp.max(kept, axis=1, keepdims=True)
        row_total = jnp.sum(jnp.exp2(kept - row_peak), axis=1, keepdims=True)
        row_lse = fold(as_row(row_peak + jnp.log2(row_total)))
        for j in range(block // lanes):
            row_ref[i * block // lanes + j : i * block // lanes + j + 1, :] = row_lse[j : j + 1, :]
        top = jnp.maximum(peak, jnp.max(kept, axis=0, keepdims=True))
        total = total * jnp.exp2(peak - top) + jnp.sum(jnp.exp2(kept - top), axis=0, keepdims=True)
        peak = top
    col_lse = by_core(fold(peak + jnp.log2(total)), where[1])
    col_ref[...] = jnp.broadcast_to(col_lse[None], col_ref.shape)
    for copy in (cols_store, *stores):
        copy.wait()


def block_stats(rows, groups, shards, n_col):
    n_rows, width = rows.shape
    n_cols = len(shards) * shards[0].shape[0]
    return pl.pallas_call(
        stats_kernel,
        in_specs=[in_hbm] * 2 + [in_vmem] * len(shards),
        out_specs=[in_hbm, in_hbm, in_hbm, in_vmem, in_vmem],
        out_shape=[
            jax.ShapeDtypeStruct((n_rows, n_cols // 2), jnp.float32),
            jax.ShapeDtypeStruct((n_rows, n_cols // 2), jnp.float32),
            jax.ShapeDtypeStruct((n_cols, width), jnp.bfloat16),
            jax.ShapeDtypeStruct((n_rows // lanes, lanes), jnp.float32),
            jax.ShapeDtypeStruct((n_col, n_cols // lanes, lanes), jnp.float32),
        ],
        scratch_shapes=[
            pltpu.VMEM((n_rows, n_cols), jnp.float32),
            pltpu.VMEM((n_rows, width), jnp.bfloat16),
            pltpu.VMEM((n_cols, width), jnp.bfloat16),
            pltpu.VMEM(groups.shape, groups.dtype),
            pltpu.SemaphoreType.DMA((3 * (n_rows // block) + 2,)),
        ],
        compiler_params=params(50),
        cost_estimate=estimate(2 * n_rows * n_cols * width, 8, 2 * n_rows * n_cols),
        name="stats",
    )(rows, groups, *shards)


def merge(parts):
    top = parts[0]
    for part in parts[1:]:
        top = jnp.maximum(top, part)
    total = jnp.exp2(parts[0] - top)
    for part in parts[1:]:
        total = total + jnp.exp2(part - top)
    return top + jnp.log2(total)


def grad_kernel(near_ref, far_ref, other_ref, cols_ref, rows_ref, other_rows_ref, row_parts, col_parts, col_others, image_ref, own_ref, *refs):
    sent, (kept, other, cols, rows, grads, other_grads, image, total, sems) = refs[:-9], refs[-9:]
    y, core, x, z = here_in_mesh()
    n_rows, n_cols = kept.shape
    half = n_cols // 2
    n_blocks = n_rows // block
    n_z = len(sent) + 1
    span = half // n_z
    per = block // lanes

    def piece(i):
        return pl.ds(i * block, block)

    loads = []
    for i in range(n_blocks):
        for side, ref in enumerate((near_ref, far_ref)):
            there = kept.at[piece(i), pl.ds(side * half, half)]
            loads.append(pltpu.make_async_copy(ref.at[piece(i), :], there, sems.at[2 * i + side]))
    at = 2 * n_blocks
    cols_load = pltpu.make_async_copy(cols_ref, cols, sems.at[at])
    other_load = pltpu.make_async_copy(other_ref, other, sems.at[at + 1])
    rows_load = pltpu.make_async_copy(rows_ref, rows.at[0], sems.at[at + 2])
    other_rows_load = pltpu.make_async_copy(other_rows_ref, rows.at[1], sems.at[at + 3])
    image_stores = [
        pltpu.make_async_copy(image.at[piece(i), :], image_ref.at[piece(i), :], sems.at[at + 4 + i])
        for i in range(n_blocks)
    ]
    for copy in (*loads[:2], cols_load, *loads[2:], rows_load, other_load, other_rows_load):
        copy.start()
    ci = col_ids((y, core, x, z), n_cols, span)
    row_lse = merge([row_parts[i, 0] for i in range(row_parts.shape[0])])
    other_lse = merge([row_parts[i, 1] for i in range(row_parts.shape[0])])
    col_lse = merge([ref[i] for ref in (col_parts, col_others) for i in range(ref.shape[0])])
    col_lse = unfold(by_core(col_lse, core))

    def gradient(logits, i, side, lse_tile, ci, col_lse):
        ri = row_ids((y, side, x, z), i * block, block, span)
        lse = as_column(unfold(lse_tile[i * per : (i + 1) * per, :]))
        weight = jnp.exp2(logits - lse) + jnp.exp2(logits - col_lse)
        grad = 0.5 * weight - jnp.where(ri == ci, 1.0, 0.0)
        return grad.astype(jnp.bfloat16)

    def fill(i):
        here = slice(i * block, (i + 1) * block)
        grads[here, :] = gradient(kept[here, :], i, core, row_lse, ci, col_lse)

    def fill_other(i):
        here = slice(i * block, (i + 1) * block)
        other_grads[here, :] = gradient(other[here, :], i, 1 - core, other_lse, ci[:, :half], col_lse[:, :half])

    loads[0].wait()
    loads[1].wait()
    fill(0)
    cols_load.wait()
    for i in range(n_blocks):
        if i + 1 < n_blocks:
            loads[2 * i + 2].wait()
            loads[2 * i + 3].wait()
            fill(i + 1)
        here = slice(i * block, (i + 1) * block)
        image[here, :] = contract(grads[here, :], cols[...], 1, 0).astype(jnp.bfloat16)
        image_stores[i].start()
    rows_load.wait()
    other_load.wait()
    for i in range(n_blocks):
        fill_other(i)
    for i in range(0, half, block):
        here = slice(i, i + block)
        total[here, :] = contract(grads[:, here], rows[0], 0, 0)
    other_rows_load.wait()
    for i in range(0, half, block):
        here = slice(i, i + block)
        total[here, :] += contract(other_grads[:, here], rows[1], 0, 0)
    for k in range(n_z):
        value = total[pl.ds(pl.multiple_of(lax.rem(z + k, n_z) * span, span), span), :]
        if k == 0:
            own_ref[...] = value
        else:
            sent[k - 1][...] = value.astype(jnp.bfloat16)
    for copy in image_stores:
        copy.wait()


def block_grad(near, far, other, cols, rows, other_rows, parts, n_z):
    n_rows, width = rows.shape
    half = near.shape[1]
    n_cols = 2 * half
    shard = (half // n_z, width)
    return pl.pallas_call(
        grad_kernel,
        in_specs=[in_hbm] * 6 + [in_vmem] * len(parts),
        out_specs=[in_hbm] + [in_vmem] * n_z,
        out_shape=[
            jax.ShapeDtypeStruct((n_rows, width), jnp.bfloat16),
            jax.ShapeDtypeStruct(shard, jnp.float32),
        ]
        + [jax.ShapeDtypeStruct(shard, jnp.bfloat16)] * (n_z - 1),
        scratch_shapes=[
            pltpu.VMEM((n_rows, n_cols), jnp.float32),
            pltpu.VMEM((n_rows, half), jnp.float32),
            pltpu.VMEM((n_cols, width), jnp.bfloat16),
            pltpu.VMEM((2, n_rows, width), jnp.bfloat16),
            pltpu.VMEM((n_rows, n_cols), jnp.bfloat16),
            pltpu.VMEM((n_rows, half), jnp.bfloat16),
            pltpu.VMEM((n_rows, width), jnp.bfloat16),
            pltpu.VMEM((half, width), jnp.float32),
            pltpu.SemaphoreType.DMA((3 * (n_rows // block) + 4,)),
        ],
        compiler_params=params(52),
        cost_estimate=estimate(4 * n_rows * n_cols * width, 14, 3 * n_rows * n_cols),
        name="grad",
    )(near, far, other, cols, rows, other_rows, *parts)


def sum_kernel(image_parts, own_ref, *refs):
    text_parts, (image_ref, text_ref, own, sem) = refs[:-4], refs[-4:]
    load = pltpu.make_async_copy(own_ref, own, sem)
    load.start()
    total = image_parts[0].astype(jnp.float32)
    for i in range(1, image_parts.shape[0]):
        total = total + image_parts[i].astype(jnp.float32)
    image_ref[...] = logit_scale * total
    total = text_parts[0][...].astype(jnp.float32)
    for ref in text_parts[1:]:
        total = total + ref[...].astype(jnp.float32)
    load.wait()
    total = total + own[...]
    text_ref[...] = logit_scale * total


def final_sums(image_parts, own, text_parts):
    n_plane, span, width = image_parts.shape
    return pl.pallas_call(
        sum_kernel,
        in_specs=[in_vmem, in_hbm] + [in_vmem] * len(text_parts),
        out_specs=[in_vmem] * 2,
        out_shape=[jax.ShapeDtypeStruct((span, width), jnp.float32)] * 2,
        scratch_shapes=[pltpu.VMEM((span, width), jnp.float32), pltpu.SemaphoreType.DMA],
        compiler_params=params(8),
        cost_estimate=estimate(span * width * 24, 4),
        name="sums",
    )(image_parts, own, *text_parts)


def per_device(image_emb, text_emb, caption_group):
    span, width = image_emb.shape
    n_y, n_core, n_x, n_z = (lax.axis_size(a) for a in axes)
    n_plane = n_y * n_x
    groups = caption_group.reshape(-1, lanes)

    rows = lax.all_to_all(repeat(image_emb, n_plane), plane, 0, 0)
    rows = rows.reshape(n_plane * span, width)
    shards = {0: text_emb}
    for k in range(1, n_z // 2):
        shards[n_z - k] = shift_z(shards[(n_z - k + 1) % n_z], 1)
        shards[k] = shift_z(shards[k - 1], -1)
    shards[n_z // 2] = shift_z(shards[n_z // 2 - 1], -1)
    near = [shards[k] for k in range(n_z)]
    far = [swap_core(shard) for shard in near]

    near_kept, far_kept, cols, row_part, col_part = block_stats(rows, groups, near + far, n_z)
    pair = jnp.stack([row_part, swap_core(row_part)])
    col_parts = lax.all_to_all(col_part, "z", 0, 0)
    row_parts = lax.all_to_all(jnp.broadcast_to(pair[None], (n_plane,) + pair.shape), plane, 0, 0)
    other_kept = swap_core(far_kept)
    other_rows = swap_core(rows)
    parts = [row_parts, col_parts, swap_core(col_parts)]

    image_part, own, *sent = block_grad(near_kept, far_kept, other_kept, cols, rows, other_rows, parts, n_z)
    image_parts = lax.all_to_all(image_part.reshape(n_plane, span, width), plane, 0, 0)
    text_parts = [shift_z(sent[k - 1], k) for k in z_steps(n_z)]
    return tuple(final_sums(image_parts, own, text_parts))


def solution(mesh):
    fine = Mesh(mesh.devices.reshape(4, 2, 4, 8), axes)
    return jax.shard_map(
        per_device,
        mesh=fine,
        in_specs=(P(axes, None), P(("x", "z", "y", "core"), None), P()),
        out_specs=(P(axes, None), P(("x", "z", "y", "core"), None)),
        check_vma=False,
    )
```

```python
import math

import jax
import jax.numpy as jnp
from jax import lax
from jax.experimental import pallas as pl
from jax.experimental.pallas import tpu as pltpu
from jax.sharding import Mesh, PartitionSpec as P

logit_scale = 100.0
scale_base2 = logit_scale / math.log(2.0)
floor_value = -1e30
mib = 1024 * 1024
lanes = 128
block = 256

axes = ("y", "core", "x", "z")
plane = ("x", "y")
in_vmem = pl.BlockSpec(memory_space=pltpu.VMEM)
in_hbm = pl.BlockSpec(memory_space=pltpu.HBM)


def swap_core(values):
    return lax.ppermute(values, "core", [(0, 1), (1, 0)])


def shift(values, axis, step):
    size = lax.axis_size(axis)
    return lax.ppermute(values, axis, [(i, (i + step) % size) for i in range(size)])


def shift_z(values, step):
    return shift(values, "z", step)


def z_steps(size):
    steps = []
    for step in range(1, size // 2):
        steps += [step, size - step]
    return steps + [size // 2]


def contract(a, b, dim_a, dim_b):
    return lax.dot_general(a, b, (((dim_a,), (dim_b,)), ((), ())), preferred_element_type=jnp.float32)


def as_column(row):
    return jnp.broadcast_to(row, (lanes, row.shape[1])).T[:, 0:1]


def as_row(column):
    return jnp.broadcast_to(column, (column.shape[0], lanes)).T[0:1, :]


def fold(row):
    return jnp.concatenate([row[:, i : i + lanes] for i in range(0, row.shape[1], lanes)], axis=0)


def unfold(tile):
    return jnp.concatenate([tile[i : i + 1, :] for i in range(tile.shape[0])], axis=1)


def by_core(tile, core):
    half = tile.shape[0] // 2
    return jnp.where(core == 0, tile, jnp.concatenate([tile[half:], tile[:half]], axis=0))


def estimate(flops, megabytes, exps=0):
    return pl.CostEstimate(flops=flops, bytes_accessed=megabytes * mib, transcendentals=exps)


def params(megabytes):
    return pltpu.CompilerParams(vmem_limit_bytes=int(megabytes * mib))


def here_in_mesh():
    return [lax.axis_index(name) for name in axes]


def row_ids(place, start, count, span):
    y, core, x, z = place
    at = start + lax.broadcasted_iota(jnp.int32, (count, 1), 0)
    member = at // span
    n_y, n_x, n_z, n_core = 4, 4, 8, 2
    return (((member % n_y * n_core + core) * n_x + member // n_y) * n_z + z) * span + at % span


def col_ids(place, count, span):
    y, core, x, z = place
    n_y, n_z, n_core = 4, 8, 2
    at = lax.broadcasted_iota(jnp.int32, (1, count), 1)
    part = at // span
    side = jnp.where(part < n_z, core, 1 - core)
    return (((x * n_z + part % n_z) * n_y + y) * n_core + side) * span + at % span


def halves(a, b, which):
    low = lax.broadcasted_iota(jnp.int32, a.shape, 1) < lanes // 2
    turned_a = jnp.where(which == 0, a, pltpu.roll(a, lanes // 2, 1))
    turned_b = jnp.where(which == 0, pltpu.roll(b, lanes // 2, 1), b)
    return jnp.where(low, turned_a, turned_b)


def group_rows(place, group_ref):
    y, core, x, z = place
    n_y, n_z, n_plane = 4, 8, 16

    def ids(at):
        return group_ref[pl.ds(at, 1), :].astype(jnp.float32)

    rows = []
    for j in range(n_plane // 2):
        a, b = [ids(((m % n_y) * 2 + core) * 16 + (m // n_y) * 4 + z // 2) for m in (2 * j, 2 * j + 1)]
        rows.append(halves(a, b, lax.rem(z, 2)))
    cols = []
    for side in (core, 1 - core):
        for j in range(n_z // 2):
            a, b = [ids((x * n_z + m) * 4 + y) for m in (2 * j, 2 * j + 1)]
            cols.append(halves(a, b, side))
    return rows, cols


def repeat_kernel(in_ref, out_ref, held, sems):
    load = pltpu.make_async_copy(in_ref, held, sems.at[0])
    load.start()
    load.wait()
    copies = [pltpu.make_async_copy(held, out_ref.at[i], sems.at[1 + i]) for i in range(out_ref.shape[0])]
    for copy in copies:
        copy.start()
    for copy in copies:
        copy.wait()


def repeat(values, count):
    return pl.pallas_call(
        repeat_kernel,
        in_specs=[in_hbm],
        out_specs=in_hbm,
        out_shape=jax.ShapeDtypeStruct((count,) + values.shape, values.dtype),
        scratch_shapes=[pltpu.VMEM(values.shape, values.dtype), pltpu.SemaphoreType.DMA((1 + count,))],
        compiler_params=params(60),
        cost_estimate=estimate(0, 2),
        name="repeat",
    )(values)


def stats_kernel(rows_ref, group_ref, *refs):
    shards, (near_ref, far_ref, cols_ref, row_ref, col_ref, kept_all, rows, cols, groups, sems) = refs[:-10], refs[-10:]
    where = here_in_mesh()
    n_rows, n_cols = kept_all.shape
    half = n_cols // 2
    n_blocks = n_rows // block
    n_z = len(shards) // 2
    span = half // n_z

    stores = []
    for i in range(n_blocks):
        for side, ref in enumerate((near_ref, far_ref)):
            here = pl.ds(i * block, block)
            there = pl.ds(side * half, half)
            stores.append(pltpu.make_async_copy(kept_all.at[here, there], ref.at[here, :], sems.at[2 * i + side]))
    cols_store = pltpu.make_async_copy(cols, cols_ref, sems.at[2 * n_blocks])
    group_load = pltpu.make_async_copy(group_ref, groups, sems.at[2 * n_blocks + 1])
    group_load.start()
    row_loads = []
    for i in range(n_blocks):
        here = pl.ds(i * block, block)
        row_loads.append(pltpu.make_async_copy(rows_ref.at[here, :], rows.at[here, :], sems.at[2 * n_blocks + 2 + i]))
        row_loads[i].start()
    for side in range(2):
        for k in range(n_z):
            at = pl.multiple_of(side * half + lax.rem(where[3] + k, n_z) * span, span)
            cols[pl.ds(at, span), :] = shards[side * n_z + k][...]
    cols_store.start()
    row_loads[0].wait()
    kept_all[:block, :] = scale_base2 * contract(rows[:block, :], cols[...], 1, 1)
    group_load.wait()
    for copy in row_loads[1:]:
        copy.wait()
    row_groups, col_groups = group_rows(where, groups)
    ci = col_ids(where, n_cols, span)
    cg = jnp.concatenate(col_groups, axis=1)

    def fill(i):
        here = slice(i * block, (i + 1) * block)
        ri = row_ids(where, i * block, block, span)
        per = block // lanes
        rg = as_column(jnp.concatenate(row_groups[i * per : (i + 1) * per], axis=1))
        scores = scale_base2 * contract(rows[here, :], cols[...], 1, 1) if i else kept_all[here, :]
        valid = jnp.logical_or(rg != cg, ri == ci)
        kept_all[here, :] = jnp.where(valid, scores, floor_value)
        stores[2 * i].start()
        stores[2 * i + 1].start()

    peak = jnp.full((1, n_cols), floor_value, jnp.float32)
    total = jnp.zeros((1, n_cols), jnp.float32)
    fill(0)
    for i in range(n_blocks):
        if i + 1 < n_blocks:
            fill(i + 1)
        kept = kept_all[i * block : (i + 1) * block, :]
        row_peak = jnp.max(kept, axis=1, keepdims=True)
        row_total = jnp.sum(jnp.exp2(kept - row_peak), axis=1, keepdims=True)
        row_lse = fold(as_row(row_peak + jnp.log2(row_total)))
        for j in range(block // lanes):
            row_ref[i * block // lanes + j : i * block // lanes + j + 1, :] = row_lse[j : j + 1, :]
        top = jnp.maximum(peak, jnp.max(kept, axis=0, keepdims=True))
        total = total * jnp.exp2(peak - top) + jnp.sum(jnp.exp2(kept - top), axis=0, keepdims=True)
        peak = top
    col_lse = by_core(fold(peak + jnp.log2(total)), where[1])
    col_ref[...] = jnp.broadcast_to(col_lse[None], col_ref.shape)
    for copy in (cols_store, *stores):
        copy.wait()


def block_stats(rows, groups, shards, n_col):
    n_rows, width = rows.shape
    n_cols = len(shards) * shards[0].shape[0]
    return pl.pallas_call(
        stats_kernel,
        in_specs=[in_hbm] * 2 + [in_vmem] * len(shards),
        out_specs=[in_hbm, in_hbm, in_hbm, in_vmem, in_vmem],
        out_shape=[
            jax.ShapeDtypeStruct((n_rows, n_cols // 2), jnp.float32),
            jax.ShapeDtypeStruct((n_rows, n_cols // 2), jnp.float32),
            jax.ShapeDtypeStruct((n_cols, width), jnp.bfloat16),
            jax.ShapeDtypeStruct((n_rows // lanes, lanes), jnp.float32),
            jax.ShapeDtypeStruct((n_col, n_cols // lanes, lanes), jnp.float32),
        ],
        scratch_shapes=[
            pltpu.VMEM((n_rows, n_cols), jnp.float32),
            pltpu.VMEM((n_rows, width), jnp.bfloat16),
            pltpu.VMEM((n_cols, width), jnp.bfloat16),
            pltpu.VMEM(groups.shape, groups.dtype),
            pltpu.SemaphoreType.DMA((3 * (n_rows // block) + 2,)),
        ],
        compiler_params=params(50),
        cost_estimate=estimate(2 * n_rows * n_cols * width, 8, 2 * n_rows * n_cols),
        name="stats",
    )(rows, groups, *shards)


def merge(parts):
    top = parts[0]
    for part in parts[1:]:
        top = jnp.maximum(top, part)
    total = jnp.exp2(parts[0] - top)
    for part in parts[1:]:
        total = total + jnp.exp2(part - top)
    return top + jnp.log2(total)


def grad_kernel(near_ref, far_ref, other_ref, cols_ref, rows_ref, other_rows_ref, row_parts, col_parts, col_others, image_ref, own_ref, *refs):
    sent, (kept, other, cols, rows, grads, other_grads, image, total, sems) = refs[:-9], refs[-9:]
    y, core, x, z = here_in_mesh()
    n_rows, n_cols = kept.shape
    half = n_cols // 2
    n_blocks = n_rows // block
    n_z = len(sent) + 1
    span = half // n_z
    per = block // lanes

    def piece(i):
        return pl.ds(i * block, block)

    loads = []
    for i in range(n_blocks):
        for side, ref in enumerate((near_ref, far_ref)):
            there = kept.at[piece(i), pl.ds(side * half, half)]
            loads.append(pltpu.make_async_copy(ref.at[piece(i), :], there, sems.at[2 * i + side]))
    at = 2 * n_blocks
    cols_load = pltpu.make_async_copy(cols_ref, cols, sems.at[at])
    other_load = pltpu.make_async_copy(other_ref, other, sems.at[at + 1])
    rows_load = pltpu.make_async_copy(rows_ref, rows.at[0], sems.at[at + 2])
    other_rows_load = pltpu.make_async_copy(other_rows_ref, rows.at[1], sems.at[at + 3])
    image_stores = [
        pltpu.make_async_copy(image.at[piece(i), :], image_ref.at[piece(i), :], sems.at[at + 4 + i])
        for i in range(n_blocks)
    ]
    for copy in (*loads[:2], cols_load, *loads[2:], rows_load, other_load, other_rows_load):
        copy.start()
    ci = col_ids((y, core, x, z), n_cols, span)
    row_lse = merge([row_parts[i, 0] for i in range(row_parts.shape[0])])
    other_lse = merge([row_parts[i, 1] for i in range(row_parts.shape[0])])
    col_lse = merge([ref[i] for ref in (col_parts, col_others) for i in range(ref.shape[0])])
    col_lse = unfold(by_core(col_lse, core))

    def gradient(logits, i, side, lse_tile, ci, col_lse):
        ri = row_ids((y, side, x, z), i * block, block, span)
        lse = as_column(unfold(lse_tile[i * per : (i + 1) * per, :]))
        weight = jnp.exp2(logits - lse) + jnp.exp2(logits - col_lse)
        grad = 0.5 * weight - jnp.where(ri == ci, 1.0, 0.0)
        return grad.astype(jnp.bfloat16)

    def fill(i):
        here = slice(i * block, (i + 1) * block)
        grads[here, :] = gradient(kept[here, :], i, core, row_lse, ci, col_lse)

    def fill_other(i):
        here = slice(i * block, (i + 1) * block)
        other_grads[here, :] = gradient(other[here, :], i, 1 - core, other_lse, ci[:, :half], col_lse[:, :half])

    loads[0].wait()
    loads[1].wait()
    fill(0)
    cols_load.wait()
    for i in range(n_blocks):
        if i + 1 < n_blocks:
            loads[2 * i + 2].wait()
            loads[2 * i + 3].wait()
            fill(i + 1)
        here = slice(i * block, (i + 1) * block)
        image[here, :] = contract(grads[here, :], cols[...], 1, 0).astype(jnp.bfloat16)
        image_stores[i].start()
    rows_load.wait()
    other_load.wait()
    for i in range(n_blocks):
        fill_other(i)
    for i in range(0, half, block):
        here = slice(i, i + block)
        total[here, :] = contract(grads[:, here], rows[0], 0, 0)
    other_rows_load.wait()
    for i in range(0, half, block):
        here = slice(i, i + block)
        total[here, :] += contract(other_grads[:, here], rows[1], 0, 0)
    for k in range(n_z):
        value = total[pl.ds(pl.multiple_of(lax.rem(z + k, n_z) * span, span), span), :]
        if k == 0:
            own_ref[...] = value
        else:
            sent[k - 1][...] = value.astype(jnp.bfloat16)
    for copy in image_stores:
        copy.wait()


def block_grad(near, far, other, cols, rows, other_rows, parts, n_z):
    n_rows, width = rows.shape
    half = near.shape[1]
    n_cols = 2 * half
    shard = (half // n_z, width)
    return pl.pallas_call(
        grad_kernel,
        in_specs=[in_hbm] * 6 + [in_vmem] * len(parts),
        out_specs=[in_hbm] + [in_vmem] * n_z,
        out_shape=[
            jax.ShapeDtypeStruct((n_rows, width), jnp.bfloat16),
            jax.ShapeDtypeStruct(shard, jnp.float32),
        ]
        + [jax.ShapeDtypeStruct(shard, jnp.bfloat16)] * (n_z - 1),
        scratch_shapes=[
            pltpu.VMEM((n_rows, n_cols), jnp.float32),
            pltpu.VMEM((n_rows, half), jnp.float32),
            pltpu.VMEM((n_cols, width), jnp.bfloat16),
            pltpu.VMEM((2, n_rows, width), jnp.bfloat16),
            pltpu.VMEM((n_rows, n_cols), jnp.bfloat16),
            pltpu.VMEM((n_rows, half), jnp.bfloat16),
            pltpu.VMEM((n_rows, width), jnp.bfloat16),
            pltpu.VMEM((half, width), jnp.float32),
            pltpu.SemaphoreType.DMA((3 * (n_rows // block) + 4,)),
        ],
        compiler_params=params(52),
        cost_estimate=estimate(4 * n_rows * n_cols * width, 14, 3 * n_rows * n_cols),
        name="grad",
    )(near, far, other, cols, rows, other_rows, *parts)


def sum_kernel(image_parts, own_ref, *refs):
    text_parts, (image_ref, text_ref, own, sem) = refs[:-4], refs[-4:]
    load = pltpu.make_async_copy(own_ref, own, sem)
    load.start()
    total = image_parts[0].astype(jnp.float32)
    for i in range(1, image_parts.shape[0]):
        total = total + image_parts[i].astype(jnp.float32)
    image_ref[...] = logit_scale * total
    total = text_parts[0][...].astype(jnp.float32)
    for ref in text_parts[1:]:
        total = total + ref[...].astype(jnp.float32)
    load.wait()
    total = total + own[...]
    text_ref[...] = logit_scale * total


def final_sums(image_parts, own, text_parts):
    n_plane, span, width = image_parts.shape
    return pl.pallas_call(
        sum_kernel,
        in_specs=[in_vmem, in_hbm] + [in_vmem] * len(text_parts),
        out_specs=[in_vmem] * 2,
        out_shape=[jax.ShapeDtypeStruct((span, width), jnp.float32)] * 2,
        scratch_shapes=[pltpu.VMEM((span, width), jnp.float32), pltpu.SemaphoreType.DMA],
        compiler_params=params(8),
        cost_estimate=estimate(span * width * 24, 4),
        name="sums",
    )(image_parts, own, *text_parts)


def per_device(image_emb, text_emb, caption_group):
    span, width = image_emb.shape
    n_y, n_core, n_x, n_z = (lax.axis_size(a) for a in axes)
    n_plane = n_y * n_x
    groups = caption_group.reshape(-1, lanes)

    rows = lax.all_to_all(repeat(image_emb, n_plane), plane, 0, 0)
    rows = rows.reshape(n_plane * span, width)
    shards = {0: text_emb}
    for k in range(1, n_z // 2):
        shards[n_z - k] = shift_z(shards[(n_z - k + 1) % n_z], 1)
        shards[k] = shift_z(shards[k - 1], -1)
    shards[n_z // 2] = shift_z(shards[n_z // 2 - 1], -1)
    near = [shards[k] for k in range(n_z)]
    far = [swap_core(shard) for shard in near]

    near_kept, far_kept, cols, row_part, col_part = block_stats(rows, groups, near + far, n_z)
    pair = jnp.stack([row_part, swap_core(row_part)])
    col_parts = lax.all_to_all(col_part, "z", 0, 0)
    row_parts = lax.all_to_all(jnp.broadcast_to(pair[None], (n_plane,) + pair.shape), plane, 0, 0)
    other_kept = swap_core(far_kept)
    other_rows = swap_core(rows)
    parts = [row_parts, col_parts, swap_core(col_parts)]

    image_part, own, *sent = block_grad(near_kept, far_kept, other_kept, cols, rows, other_rows, parts, n_z)
    image_parts = lax.all_to_all(image_part.reshape(n_plane, span, width), plane, 0, 0)
    text_parts = [shift_z(sent[k - 1], k) for k in z_steps(n_z)]
    return tuple(final_sums(image_parts, own, text_parts))


def solution(mesh):
    fine = Mesh(mesh.devices.reshape(4, 2, 4, 8), axes)
    return jax.shard_map(
        per_device,
        mesh=fine,
        in_specs=(P(axes, None), P(("x", "z", "y", "core"), None), P()),
        out_specs=(P(axes, None), P(("x", "z", "y", "core"), None)),
        check_vma=False,
    )
```
